256 devices in a mesh: seg: 16 (over z_lo, y), head: 8 (over x, core), rep: 2 (over z_hi).
Axes of the slice: x: 4, y: 4, z: 8 (z_hi: 2, z_lo: 4; z = z_hi * 4 + z_lo), core: 2. Of those that a mesh axis runs over, the one named last changes fastest.
Arguments:
- queries: bfloat16 [4096, 8192], P(('seg', 'rep'), 'head'), may hold values from -4 to 64
- criteria_keys: bfloat16 [4096, 1024], P(('seg', 'rep'), 'head'), may hold values from -8 to 40
- criteria_values: bfloat16 [4096, 1024], P(('seg', 'rep'), 'head'), may hold values from -6 to 6
- candidate_keys: bfloat16 [16384, 1024], P(('seg', 'rep'), 'head'), may hold values from -8 to 8
- candidate_values: bfloat16 [16384, 1024], P(('seg', 'rep'), 'head'), may hold values from -6 to 6
- lengths: int32 [16], replicated, may hold values from 1 to 1024, 10240 in all
- orders: int32 [16, 16], replicated, may hold values from 0 to 15, each once within a row
- out_weight: bfloat16 [8192, 8192], P('rep', 'head'), may hold values from -1 to 1
Outputs:
- projected: bfloat16 [4096, 8192], P(('seg', 'rep'), 'head')
The draws below stay inside these ranges and needn't reach their ends.
Inputs may be any that keep to these rules, and one draw needn't show every extreme that they name: `lengths`: they sum to 10240, and at least one answer fills all 1024 slots. `orders`: each row is a permutation of the answers.
All inputs are finite; a program needn't handle non-finite values.
Results may differ from the reference program's by a relative error of at most 0.013.
Values may be sent and summed in bfloat16 or wider, within the bound.
A program may use at most 128 MiB of HBM per device.

```python
import math
import jax
import jax.numpy as jnp
import numpy as np
from jax import lax

D = 8192
QUERY_HEADS = 64
KEY_VALUE_HEADS = 8
HEAD_WIDTH = 128
ANSWER_LENGTH = 1024
RUBRIC_LENGTH = 4096
ANSWER_ROWS = 256
CANDIDATE_COUNT = 16


def draw_queries(key, part):
    key = jax.random.fold_in(key, 11)
    complete_shape = (CANDIDATE_COUNT * ANSWER_ROWS, QUERY_HEADS * HEAD_WIDTH)
    sample_values = jnp.clip(jax.random.normal(key, complete_shape, jnp.float32), -4.0, 4.0)
    return sample_values.astype(jnp.bfloat16)


def draw_criteria_keys(key, part):
    key = jax.random.fold_in(key, 23)
    complete_shape = (RUBRIC_LENGTH, KEY_VALUE_HEADS * HEAD_WIDTH)
    sample_values = jnp.clip(2.0 * jax.random.normal(key, complete_shape, jnp.float32), -8.0, 8.0)
    return sample_values.astype(jnp.bfloat16)


def shard_levels(stream_key, extent, split, least, high):
    def one(dim, blocks):
        draws = jax.random.uniform(jax.random.fold_in(jax.random.fold_in(stream_key, 6), dim), (blocks,), jnp.float32, least / len(split), high / len(split))
        return jnp.repeat(jnp.exp(draws), extent[dim] // blocks).reshape((-1,) + (1,) * (len(extent) - dim - 1))

    loudness = one(*split[0])
    for cut in split[1:]:
        loudness = loudness * one(*cut)
    return loudness


def profile(count, total, most, lean):
    weights = [(1 << 20) // math.isqrt(standing ** lean) + 1 for standing in range(2, count + 1)]
    spare, given = total - most - (count - 1), [1] * (count - 1)
    while spare > 0:
        candidates = [i for i in range(count - 1) if given[i] < most]
        pool, left = sum([weights[i] for i in candidates]), spare
        for i in candidates:
            extra = min(most - given[i], max(1, left * weights[i] // pool), spare)
            given[i] = given[i] + extra
            spare = spare - extra
    return np.array([most] + given)


def ragged(key, count, total, limit, slope):
    if count == 2:
        one = jax.random.randint(key, (), max(1, total - limit), min(limit, total - 1) + 1)
        return jnp.stack([one, total - one])
    sizes = jnp.asarray(profile(count, total, limit, slope), jnp.int32)
    twos = (count - 1) // 2
    donor, sink = sizes[1:1 + 2 * twos:2], sizes[2:2 + 2 * twos:2]
    room = jnp.minimum(donor - 1, limit - sink)
    shifted = jax.random.randint(jax.random.fold_in(key, 1), (twos,), 0, 1 << 20) % (room + 1)
    sizes = sizes.at[1:1 + 2 * twos:2].set(donor - shifted).at[2:2 + 2 * twos:2].set(sink + shifted)
    return sizes[jax.random.permutation(jax.random.fold_in(key, 2), count)]


def bell_draw(rng, extent, deviation, most, shards=(), kind=jnp.bfloat16):
    drawn = deviation * jax.random.normal(rng, extent, jnp.float32)
    if shards:
        drawn = drawn * shard_levels(rng, extent, shards, -0.22, 0.18)
    return jnp.clip(drawn, -most, most).astype(kind)


def setup_inputs(seed: int = 0) -> dict:
    key_list = jax.random.split(jax.random.key(seed), 9)
    queries = draw_queries(jax.random.fold_in(key_list[8], 71), 0)
    criteria_keys = draw_criteria_keys(jax.random.fold_in(key_list[8], 71), 0)
    criteria_values = bell_draw(key_list[2], (RUBRIC_LENGTH, KEY_VALUE_HEADS * HEAD_WIDTH), 1.0, 6.0, ((0, 32), (1, 8)))
    candidate_keys = bell_draw(key_list[3], (CANDIDATE_COUNT * ANSWER_LENGTH, KEY_VALUE_HEADS * HEAD_WIDTH), 2.0, 8.0, ((0, 32), (1, 8)))
    candidate_values = bell_draw(key_list[4], (CANDIDATE_COUNT * ANSWER_LENGTH, KEY_VALUE_HEADS * HEAD_WIDTH), 1.0, 6.0, ((0, 32), (1, 8)))
    lengths = ragged(key_list[5], CANDIDATE_COUNT, 5 * CANDIDATE_COUNT * ANSWER_LENGTH // 8, ANSWER_LENGTH, 2).astype(jnp.int32)
    orders = jax.vmap(lambda own: jax.random.permutation(own, CANDIDATE_COUNT))(jax.random.split(key_list[6], CANDIDATE_COUNT)).reshape((CANDIDATE_COUNT, CANDIDATE_COUNT)).astype(jnp.int32)
    out_weight = bell_draw(key_list[7], (QUERY_HEADS * HEAD_WIDTH, D), (QUERY_HEADS * HEAD_WIDTH // 256) ** -0.5, 1.0, ((0, 2), (1, 8)))
    return dict(queries=queries, criteria_keys=criteria_keys, criteria_values=criteria_values, candidate_keys=candidate_keys, candidate_values=candidate_values, lengths=lengths, orders=orders, out_weight=out_weight)


theta_base = 1000000.0


def apply_rotary(vectors, positions):
    halfway = vectors.shape[-1] // 2
    frequency = jnp.exp(jnp.arange(halfway, dtype=jnp.float32) * (-2.0 * math.log(theta_base) / vectors.shape[-1]))
    angles = positions.astype(jnp.float32)[:, None] * frequency[None, :]
    cos_table = jnp.cos(angles)[:, None, :]
    sin_table = jnp.sin(angles)[:, None, :]
    front_half = vectors[..., :halfway]
    back_half = vectors[..., halfway:]
    return jnp.concatenate([front_half * cos_table - back_half * sin_table, back_half * cos_table + front_half * sin_table], axis=-1)


def answer_offsets(orders, lengths):
    answers = lengths.shape[0]
    placed = orders[:, :, None] == jnp.arange(answers, dtype=jnp.int32)[None, None, :]
    placed_len = jnp.sum(jnp.where(placed, lengths[None, None, :], 0), axis=2).astype(jnp.int32)
    starts = (RUBRIC_LENGTH + jnp.cumsum(placed_len, axis=1) - placed_len).astype(jnp.int32)
    return jnp.sum(jnp.where(placed, starts[:, :, None], 0), axis=1).astype(jnp.int32)


def reference(queries, criteria_keys, criteria_values, candidate_keys, candidate_values, lengths, orders, out_weight):
    query_group_count = QUERY_HEADS // KEY_VALUE_HEADS
    score_scale = HEAD_WIDTH ** -0.5
    offsets = answer_offsets(orders, lengths)
    query_pos = (RUBRIC_LENGTH + jnp.sum(lengths) + jnp.arange(ANSWER_ROWS, dtype=jnp.int32)).astype(jnp.int32)
    slot_ids = jnp.arange(CANDIDATE_COUNT * ANSWER_LENGTH, dtype=jnp.int32)
    segment = (slot_ids // ANSWER_LENGTH).astype(jnp.int32)
    within = (slot_ids - segment * ANSWER_LENGTH).astype(jnp.int32)
    live_slots = within < lengths[segment]
    live_keys = jnp.concatenate([jnp.ones((RUBRIC_LENGTH,), dtype=bool), live_slots])
    rotated_rubric = apply_rotary(criteria_keys.astype(jnp.float32).reshape(RUBRIC_LENGTH, KEY_VALUE_HEADS, HEAD_WIDTH), jnp.arange(RUBRIC_LENGTH, dtype=jnp.int32)).astype(jnp.bfloat16)
    combined_values = jnp.concatenate([criteria_values, candidate_values], axis=0).reshape(RUBRIC_LENGTH + CANDIDATE_COUNT * ANSWER_LENGTH, KEY_VALUE_HEADS, HEAD_WIDTH)
    slab_queries = queries.reshape(CANDIDATE_COUNT, ANSWER_ROWS, QUERY_HEADS, HEAD_WIDTH)
    answer_as_real = candidate_keys.astype(jnp.float32).reshape(CANDIDATE_COUNT * ANSWER_LENGTH, KEY_VALUE_HEADS, HEAD_WIDTH)

    def one_answer(answer_index):
        key_pos = (offsets[answer_index][segment] + within).astype(jnp.int32)
        answer_rot = apply_rotary(answer_as_real, key_pos).astype(jnp.bfloat16)
        keys_all = jnp.concatenate([rotated_rubric, answer_rot], axis=0)
        rotated_query = apply_rotary(slab_queries[answer_index].astype(jnp.float32), query_pos).astype(jnp.bfloat16)
        rotated_query = rotated_query.reshape(ANSWER_ROWS, KEY_VALUE_HEADS, query_group_count, HEAD_WIDTH)

        def single_head(kv_head):
            query_head = jnp.take(rotated_query, kv_head, axis=1).astype(jnp.float32)
            key_head = jnp.take(keys_all, kv_head, axis=1).astype(jnp.float32)
            value_head = jnp.take(combined_values, kv_head, axis=1).astype(jnp.float32)
            scores = jnp.einsum("sgd,kd->sgk", query_head, key_head) * score_scale
            masked = jnp.where(live_keys, scores, -jnp.inf)
            row_peak = jnp.max(masked, axis=-1, keepdims=True)
            weights = jnp.where(live_keys, jnp.exp(scores - row_peak), 0.0)
            row_total = jnp.sum(weights, axis=-1, keepdims=True)
            rounded = lax.optimization_barrier(weights.astype(jnp.bfloat16)).astype(jnp.float32)
            return jnp.einsum("sgk,kd->sgd", rounded, value_head) / row_total

        output_rows = lax.map(single_head, jnp.arange(KEY_VALUE_HEADS, dtype=jnp.int32))
        return jnp.transpose(output_rows, (1, 0, 2, 3)).reshape(ANSWER_ROWS, QUERY_HEADS * HEAD_WIDTH).astype(jnp.bfloat16)

    attended = lax.map(one_answer, jnp.arange(CANDIDATE_COUNT, dtype=jnp.int32)).reshape(CANDIDATE_COUNT * ANSWER_ROWS, QUERY_HEADS * HEAD_WIDTH)
    return jnp.dot(attended, out_weight, preferred_element_type=jnp.float32).astype(jnp.bfloat16)
```

```python
import functools
import math

import jax
import jax.numpy as jnp
import numpy as np
from jax import lax
from jax.experimental import pallas as pl
from jax.experimental.pallas import tpu as pltpu
from jax.sharding import PartitionSpec as P

QUERY_HEADS = 64
KEY_VALUE_HEADS = 8
HEAD_WIDTH = 128
ANSWER_LENGTH = 1024
RUBRIC_LENGTH = 4096
THETA = 1000000.0
GROUP = 8
ROWS = 128
SLOTS = 512
RUB = 128
SCALE = math.log2(math.e) / math.sqrt(HEAD_WIDTH)
MESH = pl.DeviceIdType.MESH
F32 = jnp.float32
BF16 = jnp.bfloat16


def tables(pos):
    halfway = HEAD_WIDTH // 2
    frequency = jnp.exp(
        jnp.arange(halfway, dtype=F32) * (-2.0 * math.log(THETA) / HEAD_WIDTH)
    )
    frequency = jnp.concatenate([frequency, frequency])
    angles = pos.astype(F32)[:, None] * frequency[None, :]
    sign = jnp.where(jnp.arange(HEAD_WIDTH) < halfway, -1.0, 1.0).astype(F32)
    return jnp.cos(angles), jnp.sin(angles) * sign[None, :]


def slot_tables():
    halfway = HEAD_WIDTH // 2
    frequency = np.exp(np.arange(halfway) * (-2.0 * math.log(THETA) / HEAD_WIDTH))
    angles = np.arange(ANSWER_LENGTH)[:, None] * frequency[None, :]
    cos, sin = np.cos(angles), np.sin(angles)
    return (
        np.concatenate([cos, cos], axis=1).astype(np.float32),
        np.concatenate([-sin, sin], axis=1).astype(np.float32),
    )


def turn(x, cos, sin):
    return x * cos + pltpu.roll(x, HEAD_WIDTH // 2, 1) * sin


def attend_kernel(
    q_ref, rk_ref, rv_ref, ck_ref, cv_ref, cos_ref, sin_ref, len_ref, jcos_ref, jsin_ref,
    att_ref,
    qbuf, rbuf, cbuf, kj, kk, vaug, acc, peak, obuf, lbuf, osend, lsend,
    qs, qr, rs, rr, cs, cr, os, orr, ls, lr,
):
    seg = lax.axis_index("seg")
    rep = lax.axis_index("rep")
    y = lax.rem(seg, 4)
    z = rep * 4 + lax.div(seg, 4)

    def at(yy, zz):
        yy = lax.rem(yy + 8, 4)
        zz = lax.rem(zz + 16, 8)
        return {"seg": lax.rem(zz, 4) * 4 + yy, "rep": lax.div(zz, 4)}

    def zs(d):
        return lax.rem(z + d + 16, 8)

    def ys(d):
        return lax.rem(y + d + 8, 4)

    def copy(src, dst, ssem, rsem, dev):
        return pltpu.make_async_remote_copy(
            src_ref=src, dst_ref=dst, send_sem=ssem, recv_sem=rsem,
            device_id=dev, device_id_type=MESH,
        )

    up, down, north, south, far = at(y, z + 1), at(y, z - 1), at(y + 1, z), at(y - 1, z), at(y + 2, z)
    barrier = pltpu.get_barrier_semaphore()
    for dev in (up, down, north, south, far):
        pl.semaphore_signal(barrier, inc=1, device_id=dev, device_id_type=MESH)
    pl.semaphore_wait(barrier, 5)

    cq, sq = cos_ref[0:128, :], sin_ref[0:128, :]
    rbuf[z, 0] = turn(rk_ref[...].astype(F32), cos_ref[128:256, :], sin_ref[128:256, :]).astype(BF16)
    rbuf[z, 1] = rv_ref[...]
    own_row = lax.broadcasted_iota(jnp.int32, (SLOTS, HEAD_WIDTH), 0) + rep * SLOTS
    own_len = len_ref[pl.ds(lax.div(seg, 4), 1), :]
    cbuf[z, 0] = ck_ref[...]
    cbuf[z, 1] = jnp.where(own_row < own_len, cv_ref[...].astype(F32), 0.0).astype(BF16)

    def ring(buf, ssem, rsem, step):
        a, b = zs(-step), zs(step)
        if step < 3:
            return (
                copy(buf.at[a], buf.at[a], ssem.at[0, step], rsem.at[0, step], up),
                copy(buf.at[b], buf.at[b], ssem.at[1, step], rsem.at[1, step], down),
            )
        return (
            copy(buf.at[a, 0], buf.at[a, 0], ssem.at[0, step], rsem.at[0, step], up),
            copy(buf.at[b, 1], buf.at[b, 1], ssem.at[1, step], rsem.at[1, step], down),
        )

    def start(pair):
        for c in pair:
            c.start()

    def arrived(pair):
        for c in pair:
            c.wait_recv()

    rub = [ring(rbuf, rs, rr, s) for s in range(4)]
    cand = [ring(cbuf, cs, cr, s) for s in range(4)]
    start(rub[0])
    start(cand[0])

    for h in range(GROUP):
        x = q_ref[:, h * 128 : (h + 1) * 128].astype(F32)
        qbuf[y, h * 128 : (h + 1) * 128, :] = turn(x, cq, sq).astype(BF16)
    qdir = (
        copy(qbuf.at[y], qbuf.at[y], qs.at[0], qr.at[0], north),
        copy(qbuf.at[y], qbuf.at[y], qs.at[1], qr.at[1], south),
    )
    start(qdir)
    south_slot, north_slot = ys(-1), ys(1)
    half = GROUP * ROWS // 2
    qfwd = (
        copy(qbuf.at[south_slot, 0:half], qbuf.at[south_slot, 0:half], qs.at[2], qr.at[2], north),
        copy(qbuf.at[north_slot, half:], qbuf.at[north_slot, half:], qs.at[3], qr.at[3], south),
    )

    arrived(rub[0])
    start(rub[1])
    arrived(rub[1])
    start(rub[2])
    arrived(qdir)
    start(qfwd)
    arrived(rub[2])
    start(rub[3])
    arrived(cand[0])
    start(cand[1])
    arrived(rub[3])

    def flash(slot, first):
        def tile(i, carry):
            rows = pl.ds(pl.multiple_of(i * 256, 256), 256)
            s = lax.dot_general(
                qbuf[slot, rows, :], kk[...], (((1,), (1,)), ((), ())), preferred_element_type=F32
            )
            top = jnp.max(s, axis=1, keepdims=True) * SCALE
            if first:
                new = jnp.broadcast_to(top, (256, 128))
            else:
                old = peak[slot, rows, :]
                new = jnp.maximum(old, top)
            p = jnp.exp2(s * SCALE - new[:, 0:1]).astype(BF16)
            o = jnp.dot(p, vaug[...], preferred_element_type=F32)
            if first:
                acc[slot, rows, :] = o
            else:
                f = jnp.exp2(old - new)
                acc[slot, rows, 0:128] = acc[slot, rows, 0:128] * f + o[:, 0:128]
                acc[slot, rows, 128:256] = acc[slot, rows, 128:256] * f + o[:, 128:256]
            peak[slot, rows, :] = new
            return carry

        lax.fori_loop(0, 4, tile, 0)

    for i in range(8):
        vaug[i * 128 : (i + 1) * 128, 0:128] = rbuf[i, 1]
        kk[i * 128 : (i + 1) * 128, :] = rbuf[i, 0]
    vaug[:, 128:256] = jnp.ones((1024, 128), BF16)
    live_key = rbuf[0, 0][0:1, :].astype(F32)

    flash(y, True)
    flash(ys(1), True)
    flash(ys(-1), True)
    arrived(qfwd)
    flash(ys(2), True)

    row = lax.broadcasted_iota(jnp.int32, (SLOTS, HEAD_WIDTH), 0)

    def live(zz):
        length = len_ref[pl.ds(lax.rem(zz, 4), 1), :]
        return row + lax.div(zz, 4) * SLOTS < length

    def prepare(pair):
        for n, zz in enumerate(pair):
            part = slice(n * SLOTS, (n + 1) * SLOTS)
            rows = pl.ds(pl.multiple_of(lax.div(zz, 4) * SLOTS, SLOTS), SLOTS)
            kj[part, :] = turn(cbuf[zz, 0].astype(F32), jcos_ref[rows, :], jsin_ref[rows, :])
            vaug[part, 0:128] = cbuf[zz, 1]
            vaug[part, 128:256] = jnp.where(live(zz), 1.0, 0.0).astype(BF16)

    def rotate(pair, slot):
        for n, zz in enumerate(pair):
            part = slice(n * SLOTS, (n + 1) * SLOTS)
            index = pl.ds(256 + slot * 4 + lax.rem(zz, 4), 1)
            k = turn(kj[part, :], cos_ref[index, :], sin_ref[index, :])
            kk[part, :] = jnp.where(live(zz), k, live_key).astype(BF16)

    def unit(pair, slot):
        rotate(pair, slot)
        flash(slot, False)

    order = (ys(2), ys(1), ys(-1), y)
    for u in range(3):
        pair = ((z, zs(1)), (zs(-1), zs(2)), (zs(-2), zs(3)))[u]
        prepare(pair)
        unit(pair, order[0])
        unit(pair, order[1])
        arrived(cand[u + 1])
        if u < 2:
            start(cand[u + 2])
        unit(pair, order[2])
        unit(pair, order[3])

    pair = (zs(-3), zs(4))
    prepare(pair)
    eye = lax.broadcasted_iota(jnp.int32, (128, 128), 0) == lax.broadcasted_iota(jnp.int32, (128, 128), 1)
    sends = []
    for n, (slot, dev) in enumerate(((ys(2), far), (ys(1), north), (ys(-1), south), (y, None))):
        unit(pair, slot)
        for h in range(GROUP):
            rows = slice(h * 128, (h + 1) * 128)
            total = acc[slot, rows, 128:256]
            mean = acc[slot, rows, 0:128] / total
            stat = peak[slot, rows, :] + jnp.log2(total)
            stat = jnp.sum(jnp.where(eye, stat, 0.0), axis=0, keepdims=True)
            osend[n, rows, :] = mean.astype(BF16)
            lsend[n, h : h + 1, :] = stat
        if dev is not None:
            pair_out = (
                copy(osend.at[n], obuf.at[n], os.at[n], orr.at[n], dev),
                copy(lsend.at[n], lbuf.at[n], ls.at[n], lr.at[n], dev),
            )
            start(pair_out)
            sends.append(pair_out)
    for pair_out in sends:
        arrived(pair_out)

    stats = [lbuf[0], lbuf[1], lbuf[2], lsend[3]]
    top = functools.reduce(jnp.maximum, stats)
    parts = [jnp.exp2(s - top) for s in stats]
    total = parts[0] + parts[1] + parts[2] + parts[3]
    shares = [p / total for p in parts]
    for h in range(GROUP):
        rows = slice(h * 128, (h + 1) * 128)
        out = None
        for n in range(4):
            w = jnp.broadcast_to(shares[n][h : h + 1, :], (128, 128)).T
            src = obuf[n, rows, :] if n < 3 else osend[3, rows, :]
            term = w * src.astype(F32)
            out = term if out is None else out + term
        att_ref[:, rows] = out.astype(BF16)

    for pairs in (rub, cand, (qdir, qfwd), sends):
        for pair in pairs:
            for c in pair:
                c.wait_send()


def project_kernel(
    att_ref, w_hbm, out_ref,
    wbuf, fbuf, part, got,
    wsem, zsend, zrecv, xs, xr, fs, fr, cs, cr, ps, pr,
):
    head = lax.axis_index("head")
    rep = lax.axis_index("rep")
    x = lax.div(head, 2)
    core = lax.rem(head, 2)
    half = lax.div(head, 4)
    mine = half == rep
    u = lax.rem(x - 2 * rep + 8, 4)
    g = lax.rem(head, 4)

    def copy(src, dst, ssem, rsem, dev):
        return pltpu.make_async_remote_copy(
            src_ref=src, dst_ref=dst, send_sem=ssem, recv_sem=rsem,
            device_id=dev, device_id_type=MESH,
        )

    load = [
        pltpu.make_async_copy(w_hbm.at[pl.ds(i * 1024, 1024)], wbuf.at[pl.ds(i * 1024, 1024)], wsem.at[i])
        for i in range(4)
    ]
    for c in load:
        c.start()
    east = {"head": lax.rem(x + 1, 4) * 2 + core}
    west = {"head": lax.rem(x + 3, 4) * 2 + core}
    other = {"head": x * 2 + 1 - core}
    partner = {"rep": 1 - rep}
    barrier = pltpu.get_barrier_semaphore()
    for dev in (east, west, other, partner):
        pl.semaphore_signal(barrier, inc=1, device_id=dev, device_id_type=MESH)
    pl.semaphore_wait(barrier, 4)

    far = 1 - rep
    swap = copy(att_ref, fbuf.at[g, rep], zsend, zrecv, partner)

    @pl.when(jnp.logical_not(mine))
    def _():
        swap.start()

    @pl.when(mine)
    def _():
        fbuf[g, rep] = att_ref[...]

    low, high = core, 2 + core

    def spread(r, n):
        blk0, blk1 = fbuf.at[low, r], fbuf.at[high, r]

        def source(blk):
            copy(blk, blk, xs.at[n, 0], xr.at[n, 0], east).start()
            copy(blk, blk, xs.at[n, 1], xr.at[n, 1], west).start()
            copy(blk, blk, cs.at[n, 0], cr.at[n, 0], other).start()

        @pl.when(u == 0)
        def _():
            source(blk0)

        @pl.when(u == 1)
        def _():
            source(blk1)

    def collect(r, n):
        blk0, blk1 = fbuf.at[low, r], fbuf.at[high, r]
        o0, o1 = fbuf.at[1 - core, r], fbuf.at[3 - core, r]

        def source_end(blk, theirs, from_east, oblk, otheirs):
            if from_east:
                copy(theirs, theirs, xs.at[n, 1], xr.at[n, 1], west).wait_recv()
            else:
                copy(theirs, theirs, xs.at[n, 0], xr.at[n, 0], east).wait_recv()
            c = copy(theirs, theirs, cs.at[n, 1], cr.at[n, 1], other)
            c.start()
            copy(blk, oblk, cs.at[n, 0], cr.at[n, 0], other).wait_recv()
            c.wait_recv()
            copy(blk, blk, xs.at[n, 0], xr.at[n, 0], east).wait_send()
            copy(blk, blk, xs.at[n, 1], xr.at[n, 1], west).wait_send()
            copy(blk, blk, cs.at[n, 0], cr.at[n, 0], other).wait_send()
            c.wait_send()

        @pl.when(u == 0)
        def _():
            source_end(blk0, blk1, True, o0, o1)

        @pl.when(u == 1)
        def _():
            source_end(blk1, blk0, False, o1, o0)

        def sink(near, other_blk, from_west):
            if from_west:
                copy(near, near, xs.at[n, 0], xr.at[n, 0], east).wait_recv()
                f = copy(near, near, fs.at[n], fr.at[n], east)
            else:
                copy(near, near, xs.at[n, 1], xr.at[n, 1], west).wait_recv()
                f = copy(near, near, fs.at[n], fr.at[n], west)
            f.start()
            c0 = copy(near, near, cs.at[n, 0], cr.at[n, 0], other)
            c0.start()
            copy(other_blk, other_blk, fs.at[n], fr.at[n], other).wait_recv()
            c1 = copy(other_blk, other_blk, cs.at[n, 1], cr.at[n, 1], other)
            c1.start()
            c0.wait_recv()
            c1.wait_recv()
            f.wait_send()
            c0.wait_send()
            c1.wait_send()

        @pl.when(u == 2)
        def _():
            sink(blk1, blk0, True)

        @pl.when(u == 3)
        def _():
            sink(blk0, blk1, False)

    spread(rep, 0)

    @pl.when(mine)
    def _():
        copy(att_ref, fbuf.at[g, far], zsend, zrecv, partner).wait_recv()

    spread(far, 1)
    collect(rep, 0)
    collect(far, 1)
    for c in load:
        c.wait()

    def product(r, columns):
        total = None
        for k in range(4):
            term = jnp.dot(
                fbuf[k, r], wbuf[k * 1024 : (k + 1) * 1024, columns], preferred_element_type=F32
            )
            total = term if total is None else total + term
        return total

    sends = []
    for j in range(4):
        columns = slice(j * 256, (j + 1) * 256)
        part[j] = product(far, columns).astype(BF16)
        c = copy(part.at[j], got.at[j], ps.at[j], pr.at[j], partner)
        c.start()
        sends.append(c)
    for j in range(4):
        columns = slice(j * 256, (j + 1) * 256)
        mine_part = product(rep, columns)
        sends[j].wait_recv()
        out_ref[:, columns] = (mine_part + got[j].astype(F32)).astype(BF16)
    for c in sends:
        c.wait_send()

    @pl.when(jnp.logical_not(mine))
    def _():
        swap.wait_send()


VMEM = pl.BlockSpec(memory_space=pltpu.VMEM)
DMA = pltpu.SemaphoreType.DMA


def local(
    queries, criteria_keys, criteria_values, candidate_keys, candidate_values,
    lengths, orders, out_weight,
):
    seg = lax.axis_index("seg")
    rep = lax.axis_index("rep")
    y, zl = lax.rem(seg, 4), lax.div(seg, 4)
    ids = jnp.arange(16, dtype=jnp.int32)
    views = lax.dynamic_slice_in_dim(orders, zl * 4, 4, 0)
    placed = views[:, :, None] == ids[None, None, :]
    placed_len = jnp.sum(jnp.where(placed, lengths[None, None, :], 0), axis=2)
    before = ids[None, :] < ids[:, None]
    starts = RUBRIC_LENGTH + jnp.sum(jnp.where(before[None], placed_len[:, None, :], 0), axis=2)
    offsets = jnp.sum(jnp.where(placed, starts[:, :, None], 0), axis=1)
    wanted = jnp.arange(4, dtype=jnp.int32) * 4 + y
    pick = wanted[:, None] == ids[None, :]
    offsets = jnp.sum(jnp.where(pick[None], offsets[:, None, :], 0), axis=2)
    mine = jnp.sum(jnp.where(pick, lengths[None, :], 0), axis=1)
    mine = jnp.broadcast_to(mine[:, None], (4, 128))
    rows = jnp.arange(ROWS, dtype=jnp.int32)
    query_pos = RUBRIC_LENGTH + jnp.sum(lengths) + rep * ROWS + rows
    rubric_pos = (seg * 2 + rep) * RUB + rows
    cos, sin = tables(jnp.concatenate([query_pos, rubric_pos, offsets.reshape(16)]))
    jcos, jsin = slot_tables()

    attended = pl.pallas_call(
        attend_kernel,
        out_shape=jax.ShapeDtypeStruct((ROWS, 1024), BF16),
        in_specs=[VMEM] * 10,
        out_specs=VMEM,
        scratch_shapes=[
            pltpu.VMEM((4, 1024, 128), BF16),
            pltpu.VMEM((8, 2, RUB, 128), BF16),
            pltpu.VMEM((8, 2, SLOTS, 128), BF16),
            pltpu.VMEM((1024, 128), F32),
            pltpu.VMEM((1024, 128), BF16),
            pltpu.VMEM((1024, 256), BF16),
            pltpu.VMEM((4, 1024, 256), F32),
            pltpu.VMEM((4, 1024, 128), F32),
            pltpu.VMEM((3, 1024, 128), BF16),
            pltpu.VMEM((3, 8, 128), F32),
            pltpu.VMEM((4, 1024, 128), BF16),
            pltpu.VMEM((4, 8, 128), F32),
            DMA((4,)), DMA((4,)),
            DMA((2, 4)), DMA((2, 4)),
            DMA((2, 4)), DMA((2, 4)),
            DMA((3,)), DMA((3,)),
            DMA((3,)), DMA((3,)),
        ],
        compiler_params=pltpu.CompilerParams(
            collective_id=0, has_side_effects=True, vmem_limit_bytes=48 * 1024 * 1024
        ),
        name="attend",
    )(
        queries, criteria_keys, criteria_values, candidate_keys, candidate_values,
        cos, sin, mine, jnp.asarray(jcos), jnp.asarray(jsin),
    )
    return pl.pallas_call(
        project_kernel,
        out_shape=jax.ShapeDtypeStruct((ROWS, 1024), BF16),
        in_specs=[VMEM, pl.BlockSpec(memory_space=pl.ANY)],
        out_specs=VMEM,
        scratch_shapes=[
            pltpu.VMEM((4096, 1024), BF16),
            pltpu.VMEM((4, 2, ROWS, 1024), BF16),
            pltpu.VMEM((4, ROWS, 256), BF16),
            pltpu.VMEM((4, ROWS, 256), BF16),
            DMA((4,)),
            DMA, DMA,
            DMA((2, 2)), DMA((2, 2)),
            DMA((2,)), DMA((2,)),
            DMA((2, 2)), DMA((2, 2)),
            DMA((4,)), DMA((4,)),
        ],
        compiler_params=pltpu.CompilerParams(
            collective_id=1, has_side_effects=True, vmem_limit_bytes=48 * 1024 * 1024
        ),
        name="project",
    )(attended, out_weight)


def solution(mesh):
    rows = P(("seg", "rep"), "head")
    return jax.shard_map(
        local,
        mesh=mesh,
        in_specs=(rows, rows, rows, rows, rows, P(), P(), P("rep", "head")),
        out_specs=rows,
        check_vma=False,
    )
```

```python
import functools
import math

import jax
import jax.numpy as jnp
import numpy as np
from jax import lax
from jax.experimental import pallas as pl
from jax.experimental.pallas import tpu as pltpu
from jax.sharding import PartitionSpec as P

QUERY_HEADS = 64
KEY_VALUE_HEADS = 8
HEAD_WIDTH = 128
ANSWER_LENGTH = 1024
RUBRIC_LENGTH = 4096
THETA = 1000000.0
GROUP = 8
ROWS = 128
SLOTS = 512
RUB = 128
CHUNK = 64
SCALE = math.log2(math.e) / math.sqrt(HEAD_WIDTH)
MESH = pl.DeviceIdType.MESH
F32 = jnp.float32
BF16 = jnp.bfloat16


def tables(pos):
    halfway = HEAD_WIDTH // 2
    frequency = jnp.exp(
        jnp.arange(halfway, dtype=F32) * (-2.0 * math.log(THETA) / HEAD_WIDTH)
    )
    frequency = jnp.concatenate([frequency, frequency])
    angles = pos.astype(F32)[:, None] * frequency[None, :]
    sign = jnp.where(jnp.arange(HEAD_WIDTH) < halfway, -1.0, 1.0).astype(F32)
    return jnp.cos(angles), jnp.sin(angles) * sign[None, :]


def slot_tables():
    halfway = HEAD_WIDTH // 2
    frequency = np.exp(np.arange(halfway) * (-2.0 * math.log(THETA) / HEAD_WIDTH))
    angles = np.arange(ANSWER_LENGTH)[:, None] * frequency[None, :]
    cos, sin = np.cos(angles), np.sin(angles)
    return (
        np.concatenate([cos, cos], axis=1).astype(np.float32),
        np.concatenate([-sin, sin], axis=1).astype(np.float32),
    )


def turn(x, cos, sin):
    return x * cos + pltpu.roll(x, HEAD_WIDTH // 2, 1) * sin


def fused_kernel(
    q_ref, rk_ref, rv_ref, ck_ref, cv_ref, cos_ref, sin_ref, len_ref, jcos_ref, jsin_ref, w_ref,
    out_ref,
    qin, rkin, cvin, cost, sint, lens, jcos, jsin, ocos, osin,
    qbuf, rbuf, cbuf, kjt, kkt, vaug, live_col, acc, peak, obuf, lbuf, osend, lsend,
    wbuf, fbuf, att, part, got,
    ins, ws, qs, qr, rs, rr, cs, cr, os, orr, ls, lr,
    zsend, zrecv, xs, xr, fs, fr, ds, dr, ps, pr,
):
    seg = lax.axis_index("seg")
    rep = lax.axis_index("rep")
    head = lax.axis_index("head")
    y = lax.rem(seg, 4)
    z = rep * 4 + lax.div(seg, 4)
    x = lax.div(head, 2)
    core = lax.rem(head, 2)

    def at(yy, zz):
        yy = lax.rem(yy + 8, 4)
        zz = lax.rem(zz + 16, 8)
        return {"seg": lax.rem(zz, 4) * 4 + yy, "rep": lax.div(zz, 4)}

    def zs(d):
        return lax.rem(z + d + 16, 8)

    def ys(d):
        return lax.rem(y + d + 8, 4)

    def copy(src, dst, ssem, rsem, dev):
        return pltpu.make_async_remote_copy(
            src_ref=src, dst_ref=dst, send_sem=ssem, recv_sem=rsem,
            device_id=dev, device_id_type=MESH,
        )

    def start(pair):
        for c in pair:
            c.start()

    def arrived(pair):
        for c in pair:
            c.wait_recv()

    load = [
        pltpu.make_async_copy(a, b, ins.at[i])
        for i, (a, b) in enumerate((
            (rk_ref, rkin), (rv_ref, rbuf.at[z, 1]), (cos_ref, cost), (sin_ref, sint),
            (cv_ref, cvin), (ck_ref, cbuf.at[z, 0]), (len_ref, lens), (q_ref, qin),
            (jcos_ref, jcos), (jsin_ref, jsin),
        ))
    ]
    start(load)

    up, down = at(y, z + 1), at(y, z - 1)
    north, south, beyond = at(y + 1, z), at(y - 1, z), at(y + 2, z)
    east = {"head": lax.rem(x + 1, 4) * 2 + core}
    west = {"head": lax.rem(x + 3, 4) * 2 + core}
    other = {"head": x * 2 + 1 - core}
    partner = {"rep": 1 - rep}
    barrier = pltpu.get_barrier_semaphore()
    peers = (up, down, north, south, beyond, east, west, other, partner)
    for dev in peers:
        pl.semaphore_signal(barrier, inc=1, device_id=dev, device_id_type=MESH)
    pl.semaphore_wait(barrier, len(peers))

    def ring(buf, ssem, rsem, step):
        a, b = zs(-step), zs(step)
        if step < 3:
            return (
                copy(buf.at[a], buf.at[a], ssem.at[0, step], rsem.at[0, step], up),
                copy(buf.at[b], buf.at[b], ssem.at[1, step], rsem.at[1, step], down),
            )
        return (
            copy(buf.at[a, 0], buf.at[a, 0], ssem.at[0, step], rsem.at[0, step], up),
            copy(buf.at[b, 1], buf.at[b, 1], ssem.at[1, step], rsem.at[1, step], down),
        )

    rub = [ring(rbuf, rs, rr, s) for s in range(4)]
    cand = [ring(cbuf, cs, cr, s) for s in range(4)]
    for c in load[:4]:
        c.wait()
    rbuf[z, 0] = turn(rkin[...].astype(F32), cost[128:256, :], sint[128:256, :]).astype(BF16)
    start(rub[0])
    for c in load[4:7]:
        c.wait()
    own_row = lax.broadcasted_iota(jnp.int32, (SLOTS, HEAD_WIDTH), 0) + rep * SLOTS
    own_len = lens[pl.ds(lax.div(seg, 4), 1), :]
    cbuf[z, 1] = jnp.where(own_row < own_len, cvin[...].astype(F32), 0.0).astype(BF16)
    start(cand[0])
    load[7].wait()
    cq, sq = cost[0:128, :], sint[0:128, :]
    for h in range(GROUP):
        v = qin[:, h * 128 : (h + 1) * 128].astype(F32)
        qbuf[y, h * 128 : (h + 1) * 128, :] = turn(v, cq, sq).astype(BF16)
    qdir = (
        copy(qbuf.at[y], qbuf.at[y], qs.at[0], qr.at[0], north),
        copy(qbuf.at[y], qbuf.at[y], qs.at[1], qr.at[1], south),
    )
    start(qdir)
    south_slot, north_slot = ys(-1), ys(1)
    mid = GROUP * ROWS // 2
    qfwd = (
        copy(qbuf.at[south_slot, 0:mid], qbuf.at[south_slot, 0:mid], qs.at[2], qr.at[2], north),
        copy(qbuf.at[north_slot, mid:], qbuf.at[north_slot, mid:], qs.at[3], qr.at[3], south),
    )
    wload = [
        pltpu.make_async_copy(w_ref.at[pl.ds(i * 1024, 1024)], wbuf.at[pl.ds(i * 1024, 1024)], ws.at[i])
        for i in range(4)
    ]
    start(wload)

    arrived(rub[0])
    start(rub[1])
    for i in range(16):
        ocos[i] = jnp.broadcast_to(cost[256 + i : 257 + i, :], (128, 128)).T
        osin[i] = jnp.broadcast_to(sint[256 + i : 257 + i, :], (128, 128)).T
    arrived(rub[1])
    start(rub[2])
    arrived(qdir)
    start(qfwd)
    load[8].wait()
    load[9].wait()
    arrived(rub[2])
    start(rub[3])
    arrived(cand[0])
    start(cand[1])

    lane = lax.broadcasted_iota(jnp.int32, (1, 128), 1)
    row = lax.broadcasted_iota(jnp.int32, (SLOTS, HEAD_WIDTH), 0)

    def prepare(shards, base):
        for n, zz in enumerate(shards):
            part_rows = slice(base + n * SLOTS, base + (n + 1) * SLOTS)
            place = lax.div(zz, 4) * SLOTS
            rows = pl.ds(pl.multiple_of(place, SLOTS), SLOTS)
            kjt[:, part_rows] = turn(cbuf[zz, 0].astype(F32), jcos[rows, :], jsin[rows, :]).T
            vaug[part_rows, 0:128] = cbuf[zz, 1]
            alive = row + place < lens[pl.ds(lax.rem(zz, 4), 1), :]
            vaug[part_rows, 128:256] = jnp.where(alive, 1.0, 0.0).astype(BF16)

    def rotate(shards, base, slot):
        for n, zz in enumerate(shards):
            length = lens[pl.ds(lax.rem(zz, 4), 1), :]
            place = lax.div(zz, 4) * SLOTS
            co, so = ocos[slot * 4 + lax.rem(zz, 4)], osin[slot * 4 + lax.rem(zz, 4)]
            for i in range(SLOTS // 128):
                cols = slice(base + n * SLOTS + i * 128, base + n * SLOTS + (i + 1) * 128)
                k = kjt[:, cols]
                k = k * co + jnp.concatenate([k[64:], k[:64]], axis=0) * so
                alive = lane + (place + i * 128) < length
                kkt[:, cols] = jnp.where(alive, k, live_col[...]).astype(BF16)

    def flash(slot, keys, first):
        scores = [
            jnp.dot(qbuf[slot, i * 256 : (i + 1) * 256, :], kkt[:, 0:keys], preferred_element_type=F32)
            for i in range(4)
        ]
        for i in range(4):
            rows = slice(i * 256, (i + 1) * 256)
            s = scores[i]
            top = jnp.max(s, axis=1, keepdims=True) * SCALE
            if first:
                new = jnp.broadcast_to(top, (256, 128))
            else:
                old = peak[slot, rows, :]
                new = jnp.maximum(old, top)
            p = jnp.exp2(s * SCALE - new[:, 0:1]).astype(BF16)
            o = jnp.dot(p, vaug[0:keys, :], preferred_element_type=F32)
            if first:
                acc[slot, rows, :] = o
            else:
                f = jnp.exp2(old - new)
                acc[slot, rows, 0:128] = acc[slot, rows, 0:128] * f + o[:, 0:128]
                acc[slot, rows, 128:256] = acc[slot, rows, 128:256] * f + o[:, 128:256]
            peak[slot, rows, :] = new

    shards = (z, zs(1))
    prepare(shards, 1024)
    arrived(rub[3])
    for i in range(8):
        vaug[i * 128 : (i + 1) * 128, 0:128] = rbuf[i, 1]
        kkt[:, i * 128 : (i + 1) * 128] = rbuf[i, 0].astype(F32).T.astype(BF16)
    vaug[0:1024, 128:256] = jnp.ones((1024, 128), BF16)
    live_col[...] = jnp.broadcast_to(rbuf[0, 0][0:1, :].astype(F32), (128, 128)).T

    def unit0(n, carry):
        slot = lax.rem(y + 3 * n, 4)

        @pl.when(n == 2)
        def _():
            arrived(qfwd)
            arrived(cand[1])
            start(cand[2])

        rotate(shards, 1024, slot)
        flash(slot, 2048, True)
        return carry

    lax.fori_loop(0, 4, unit0, 0)

    arrived(cand[2])
    start(cand[3])
    shards1 = (zs(-1), zs(2), zs(-2), zs(3))
    prepare(shards1, 0)

    def unit1(n, carry):
        slot = lax.rem(y + 2 + 3 * n, 4)
        rotate(shards1, 0, slot)
        flash(slot, 2048, False)
        return carry

    lax.fori_loop(0, 4, unit1, 0)

    arrived(cand[3])
    shards2 = (zs(-3), zs(4))
    prepare(shards2, 0)
    eye = lax.broadcasted_iota(jnp.int32, (128, 128), 0) == lax.broadcasted_iota(jnp.int32, (128, 128), 1)

    def outgoing(n, dev):
        return (
            copy(osend.at[n], obuf.at[n], os.at[n], orr.at[n], dev),
            copy(lsend.at[n], lbuf.at[n], ls.at[n], lr.at[n], dev),
        )

    def unit2(n, carry):
        slot = lax.rem(y + 2 + 3 * n, 4)
        rotate(shards2, 0, slot)
        flash(slot, 1024, False)
        for h in range(GROUP):
            rows = slice(h * 128, (h + 1) * 128)
            total = acc[slot, rows, 128:256]
            stat = peak[slot, rows, :] + jnp.log2(total)
            osend[n, rows, :] = (acc[slot, rows, 0:128] / total).astype(BF16)
            lsend[n, h : h + 1, :] = jnp.sum(jnp.where(eye, stat, 0.0), axis=0, keepdims=True)

        @pl.when(n != 2)
        def _():
            start(outgoing(n, at(slot, z)))

        return carry

    lax.fori_loop(0, 4, unit2, 0)
    partials = [outgoing(0, beyond), outgoing(1, north), outgoing(3, south)]
    for pair in partials:
        arrived(pair)

    half = lax.div(head, 4)
    mine = half == rep
    u = lax.rem(x - 2 * rep + 8, 4)
    g = lax.rem(head, 4)
    far = 1 - rep

    stats = [lbuf[0], lbuf[1], lsend[2], lbuf[3]]
    top = functools.reduce(jnp.maximum, stats)
    parts = [jnp.exp2(s - top) for s in stats]
    total = parts[0] + parts[1] + parts[2] + parts[3]
    shares = [p / total for p in parts]
    for h in range(GROUP):
        rows = slice(h * 128, (h + 1) * 128)
        out = None
        for n in range(4):
            w = jnp.broadcast_to(shares[n][h : h + 1, :], (128, 128)).T
            src = osend[2, rows, :] if n == 2 else obuf[n, rows, :]
            term = w * src.astype(F32)
            out = term if out is None else out + term
        att[:, rows] = out.astype(BF16)

    @pl.when(mine)
    def _():
        fbuf[g, rep] = att[...]

    def chunk(i):
        return pl.ds(i * CHUNK, CHUNK)

    swaps = [
        copy(att.at[chunk(i)], fbuf.at[g, rep, chunk(i)], zsend.at[i], zrecv.at[i], partner)
        for i in range(2)
    ]
    swapped = [
        copy(fbuf.at[g, far, chunk(i)], fbuf.at[g, far, chunk(i)], zsend.at[i], zrecv.at[i], partner)
        for i in range(2)
    ]
    items = [(rep, pl.ds(0, ROWS)), (far, chunk(0)), (far, chunk(1))]

    def block(k, n):
        r, rows = items[n]
        return fbuf.at[k, r, rows]

    def hop(blk, n, way):
        return copy(blk, blk, xs.at[n, way], xr.at[n, way], (east, west)[way])

    def cross(blk, n, way):
        return copy(blk, blk, ds.at[n, way], dr.at[n, way], other)

    def source(k, k_other, way_in):
        def send(n):
            start((hop(block(k, n), n, 0), hop(block(k, n), n, 1), cross(block(k, n), n, 0)))

        send(0)
        for i in range(2):
            swapped[i].wait_recv()
            send(i + 1)
        for n in range(3):
            hop(block(k_other, n), n, way_in).wait_recv()
            cross(block(k_other, n), n, 1).start()

    def source_end(n, k, k_other):
        cross(block(k, n), n, 0).wait_recv()
        cross(block(k_other, n), n, 1).wait_recv()

    def sink(k_near, k_far, way):
        start(swaps)
        for n in range(3):
            near = block(k_near, n)
            hop(near, n, way).wait_recv()
            start((copy(near, near, fs.at[n], fr.at[n], (east, west)[way]), cross(near, n, 0)))
            if n:
                pass_on(k_near, k_far, way, n - 1)
        pass_on(k_near, k_far, way, 2)

    def pass_on(k_near, k_far, way, n):
        blk = block(k_far, n)
        copy(blk, blk, fs.at[n], fr.at[n], (east, west)[way]).wait_recv()
        cross(blk, n, 1).start()

    low, high = core, 2 + core
    roles = ((0, low, high), (1, high, low), (2, high, low), (3, low, high))
    for which, k0, k1 in roles:

        @pl.when(u == which)
        def _():
            if which < 2:
                source(k0, k1, 1 - which)
            else:
                sink(k0, k1, which - 2)

    for c in wload:
        c.wait()

    def crossed(n):
        r, rows = items[n]
        blk = fbuf.at[g, r, rows]
        cross(blk, n, 0).wait_recv()
        cross(blk, n, 1).wait_recv()

    def product(r, rows):
        total = None
        for k in range(4):
            term = jnp.dot(
                fbuf[k, r, rows, :], wbuf[k * 1024 : (k + 1) * 1024, :], preferred_element_type=F32
            )
            total = term if total is None else total + term
        return total

    sends = []
    for i in range(2):
        rows = slice(i * CHUNK, (i + 1) * CHUNK)
        crossed(i + 1)
        part[rows, :] = product(far, rows).astype(BF16)
        c = copy(part.at[chunk(i)], got.at[chunk(i)], ps.at[i], pr.at[i], partner)
        c.start()
        sends.append(c)
    crossed(0)
    own = product(rep, slice(0, ROWS))
    for i in range(2):
        rows = slice(i * CHUNK, (i + 1) * CHUNK)
        sends[i].wait_recv()
        out_ref[rows, :] = (own[rows, :] + got[rows, :].astype(F32)).astype(BF16)

    for pairs in (rub, cand, (qdir, qfwd), partials, (sends,)):
        for pair in pairs:
            for c in pair:
                c.wait_send()
    for n in range(3):
        blk = block(g, n)
        cross(blk, n, 0).wait_send()
        cross(blk, n, 1).wait_send()

    @pl.when(mine)
    def _():
        for n in range(3):
            hop(block(g, n), n, 0).wait_send()
            hop(block(g, n), n, 1).wait_send()

    @pl.when(jnp.logical_not(mine))
    def _():
        for n in range(3):
            blk = block(g, n)
            copy(blk, blk, fs.at[n], fr.at[n], east).wait_send()
        for c in swaps:
            c.wait_send()


VMEM = pl.BlockSpec(memory_space=pltpu.VMEM)
ANY = pl.BlockSpec(memory_space=pl.ANY)
DMA = pltpu.SemaphoreType.DMA


def local(
    queries, criteria_keys, criteria_values, candidate_keys, candidate_values,
    lengths, orders, out_weight,
):
    seg = lax.axis_index("seg")
    rep = lax.axis_index("rep")
    y, zl = lax.rem(seg, 4), lax.div(seg, 4)
    ids = jnp.arange(16, dtype=jnp.int32)
    views = lax.dynamic_slice_in_dim(orders, zl * 4, 4, 0)
    placed = views[:, :, None] == ids[None, None, :]
    placed_len = jnp.sum(jnp.where(placed, lengths[None, None, :], 0), axis=2)
    before = ids[None, :] < ids[:, None]
    starts = RUBRIC_LENGTH + jnp.sum(jnp.where(before[None], placed_len[:, None, :], 0), axis=2)
    offsets = jnp.sum(jnp.where(placed, starts[:, :, None], 0), axis=1)
    wanted = jnp.arange(4, dtype=jnp.int32) * 4 + y
    pick = wanted[:, None] == ids[None, :]
    offsets = jnp.sum(jnp.where(pick[None], offsets[:, None, :], 0), axis=2)
    mine = jnp.sum(jnp.where(pick, lengths[None, :], 0), axis=1)
    mine = jnp.broadcast_to(mine[:, None], (4, 128))
    rows = jnp.arange(ROWS, dtype=jnp.int32)
    query_pos = RUBRIC_LENGTH + jnp.sum(lengths) + rep * ROWS + rows
    rubric_pos = (seg * 2 + rep) * RUB + rows
    cos, sin = tables(jnp.concatenate([query_pos, rubric_pos, offsets.reshape(16)]))
    jcos, jsin = slot_tables()

    V = pltpu.VMEM
    return pl.pallas_call(
        fused_kernel,
        out_shape=jax.ShapeDtypeStruct((ROWS, 1024), BF16),
        in_specs=[ANY] * 11,
        out_specs=VMEM,
        scratch_shapes=[
            V((ROWS, 1024), BF16), V((RUB, 128), BF16), V((SLOTS, 128), BF16),
            V((272, 128), F32), V((272, 128), F32), V((4, 128), jnp.int32),
            V((1024, 128), F32), V((1024, 128), F32),
            V((16, 128, 128), F32), V((16, 128, 128), F32),
            V((4, 1024, 128), BF16), V((8, 2, RUB, 128), BF16), V((8, 2, SLOTS, 128), BF16),
            V((128, 2048), F32), V((128, 2048), BF16), V((2048, 256), BF16), V((128, 128), F32),
            V((4, 1024, 256), F32), V((4, 1024, 128), F32),
            V((4, 1024, 128), BF16), V((4, 8, 128), F32),
            V((4, 1024, 128), BF16), V((4, 8, 128), F32),
            V((4096, 1024), BF16), V((4, 2, ROWS, 1024), BF16),
            V((ROWS, 1024), BF16), V((ROWS, 1024), BF16), V((ROWS, 1024), BF16),
            DMA((10,)), DMA((4,)),
            DMA((4,)), DMA((4,)),
            DMA((2, 4)), DMA((2, 4)),
            DMA((2, 4)), DMA((2, 4)),
            DMA((4,)), DMA((4,)),
            DMA((4,)), DMA((4,)),
            DMA((2,)), DMA((2,)),
            DMA((3, 2)), DMA((3, 2)),
            DMA((3,)), DMA((3,)),
            DMA((3, 2)), DMA((3, 2)),
            DMA((2,)), DMA((2,)),
        ],
        compiler_params=pltpu.CompilerParams(
            collective_id=0, has_side_effects=True, vmem_limit_bytes=58 * 1024 * 1024
        ),
        name="judge",
    )(
        queries, criteria_keys, criteria_values, candidate_keys, candidate_values,
        cos, sin, mine, jnp.asarray(jcos), jnp.asarray(jsin), out_weight,
    )


def solution(mesh):
    rows = P(("seg", "rep"), "head")
    return jax.shard_map(
        local,
        mesh=mesh,
        in_specs=(rows, rows, rows, rows, rows, P(), P(), P("rep", "head")),
        out_specs=rows,
        check_vma=False,
    )
```

```python
import functools
import math

import jax
import jax.numpy as jnp
import numpy as np
from jax import lax
from jax.experimental import pallas as pl
from jax.experimental.pallas import tpu as pltpu
from jax.sharding import PartitionSpec as P

QUERY_HEADS = 64
KEY_VALUE_HEADS = 8
HEAD_WIDTH = 128
ANSWER_LENGTH = 1024
RUBRIC_LENGTH = 4096
THETA = 1000000.0
GROUP = 8
ROWS = 128
SLOTS = 512
RUB = 128
CHUNK = 64
LIVE_TOTAL = 10240
QUERY_START = RUBRIC_LENGTH + LIVE_TOTAL
SHARD = SLOTS + RUB
HALF = GROUP * CHUNK
SCALE = math.log2(math.e) / math.sqrt(HEAD_WIDTH)
MESH = pl.DeviceIdType.MESH
F32 = jnp.float32
BF16 = jnp.bfloat16


def tables(pos):
    halfway = HEAD_WIDTH // 2
    frequency = jnp.exp(
        jnp.arange(halfway, dtype=F32) * (-2.0 * math.log(THETA) / HEAD_WIDTH)
    )
    frequency = jnp.concatenate([frequency, frequency])
    angles = pos.astype(F32)[:, None] * frequency[None, :]
    sign = jnp.where(jnp.arange(HEAD_WIDTH) < halfway, -1.0, 1.0).astype(F32)
    return jnp.cos(angles), jnp.sin(angles) * sign[None, :]


def angle_tables():
    halfway = HEAD_WIDTH // 2
    exponent = np.arange(halfway, dtype=np.float32) * np.float32(-2.0 * math.log(THETA) / HEAD_WIDTH)
    frequency = np.exp(exponent).astype(np.float32)
    positions = np.concatenate([
        np.arange(RUBRIC_LENGTH), QUERY_START + np.arange(2 * ROWS),     ]).astype(np.float32)
    angles = (positions[:, None] * frequency[None, :]).astype(np.float64)
    cos, sin = np.cos(angles), np.sin(angles)
    return (
        np.concatenate([cos, cos], axis=1).astype(np.float32),
        np.concatenate([-sin, sin], axis=1).astype(np.float32),
    )


def turn(x, cos, sin):
    return x * cos + pltpu.roll(x, HEAD_WIDTH // 2, 1) * sin


def fused_kernel(
    q_ref, rk_ref, rv_ref, ck_ref, cv_ref, cos_ref, sin_ref, w_ref, len_ref, hcos_ref, hsin_ref,
    out_ref,
    lens, qin, cvin, rvin, ckin, rkin, jcos, jsin, hcos, hsin, qcos, qsin, rcos, rsin, ocos, osin,
    qbuf, kbuf, vbuf, kjt, kkt, vaug, live_col, acc, peak, obuf, lbuf, osend, lsend,
    wbuf, fbuf, att, part, got,
    ins, ws, qs, qr, cs, cr, os, orr, ls, lr,
    zsend, zrecv, xs, xr, fs, fr, ds, dr, ps, pr,
):
    seg = lax.axis_index("seg")
    rep = lax.axis_index("rep")
    head = lax.axis_index("head")
    y = lax.rem(seg, 4)
    zl = lax.div(seg, 4)
    z = rep * 4 + zl
    x = lax.div(head, 2)
    core = lax.rem(head, 2)

    def at(yy, zz):
        yy = lax.rem(yy + 8, 4)
        zz = lax.rem(zz + 16, 8)
        return {"seg": lax.rem(zz, 4) * 4 + yy, "rep": lax.div(zz, 4)}

    def zs(d):
        return lax.rem(z + d + 16, 8)

    def ys(d):
        return lax.rem(y + d + 8, 4)

    def copy(src, dst, ssem, rsem, dev):
        return pltpu.make_async_remote_copy(
            src_ref=src, dst_ref=dst, send_sem=ssem, recv_sem=rsem,
            device_id=dev, device_id_type=MESH,
        )

    def start(pair):
        for c in pair:
            c.start()

    def arrived(pair):
        for c in pair:
            c.wait_recv()

    mine_rows = pl.ds((seg * 2 + rep) * RUB, RUB)
    query_rows = pl.ds(RUBRIC_LENGTH + rep * ROWS, ROWS)
    low_rows = pl.ds(0, 1024)
    load = [
        pltpu.make_async_copy(a, b, ins.at[i])
        for i, (a, b) in enumerate((
            (cv_ref, cvin), (rv_ref, rvin),
            (q_ref, qin), (cos_ref.at[query_rows], qcos), (sin_ref.at[query_rows], qsin),
            (ck_ref, ckin), (rk_ref, rkin),
            (cos_ref.at[mine_rows], rcos), (sin_ref.at[mine_rows], rsin),
            (hcos_ref, hcos), (hsin_ref, hsin), (len_ref, lens),
            (cos_ref.at[low_rows], jcos), (sin_ref.at[low_rows], jsin),
        ))
    ]
    start(load)

    up, down = at(y, z + 1), at(y, z - 1)
    north, south, beyond = at(y + 1, z), at(y - 1, z), at(y + 2, z)
    east = {"head": lax.rem(x + 1, 4) * 2 + core}
    west = {"head": lax.rem(x + 3, 4) * 2 + core}
    other = {"head": x * 2 + 1 - core}
    partner = {"rep": 1 - rep}
    barrier = pltpu.get_barrier_semaphore()
    peers = (up, down, north, south, beyond, east, west, other, partner)
    for dev in peers:
        pl.semaphore_signal(barrier, inc=1, device_id=dev, device_id_type=MESH)
    pl.semaphore_wait(barrier, len(peers))

    def ring(step, c):
        a, b = zs(-step), zs(step)
        buf = (kbuf, vbuf)[c]
        ahead = copy(buf.at[a], buf.at[a], cs.at[0, step * 2 + c], cr.at[0, step * 2 + c], up)
        back = copy(buf.at[b], buf.at[b], cs.at[1, step * 2 + c], cr.at[1, step * 2 + c], down)
        if step < 3:
            return (ahead, back)
        return (ahead,) if c == 1 else (back,)

    rings = [[ring(s, c) for c in range(2)] for s in range(4)]

    def forward(step, c):
        arrived(rings[step][c])
        start(rings[step + 1][c])

    for c in load[:2]:
        c.wait()
    vbuf[z, 0:SLOTS, :] = cvin[...]
    vbuf[z, SLOTS:SHARD, :] = rvin[...]
    start(rings[0][1])
    for c in load[2:5]:
        c.wait()
    cq, sq = qcos[...], qsin[...]
    for h in range(GROUP):
        v = turn(qin[:, h * 128 : (h + 1) * 128].astype(F32), cq, sq).astype(BF16)
        qbuf[y, h * CHUNK : (h + 1) * CHUNK, :] = v[:CHUNK]
        qbuf[y, HALF + h * CHUNK : HALF + (h + 1) * CHUNK, :] = v[CHUNK:]
    qdir = (
        copy(qbuf.at[y], qbuf.at[y], qs.at[0], qr.at[0], north),
        copy(qbuf.at[y], qbuf.at[y], qs.at[1], qr.at[1], south),
    )
    start(qdir)
    for c in load[5:9]:
        c.wait()
    kbuf[z, 0:SLOTS, :] = ckin[...]
    kbuf[z, SLOTS:SHARD, :] = turn(rkin[...].astype(F32), rcos[...], rsin[...]).astype(BF16)
    start(rings[0][0])
    south_slot, north_slot = ys(-1), ys(1)
    qfwd = (
        copy(qbuf.at[south_slot, 0:HALF], qbuf.at[south_slot, 0:HALF], qs.at[2], qr.at[2], north),
        copy(qbuf.at[north_slot, HALF:], qbuf.at[north_slot, HALF:], qs.at[3], qr.at[3], south),
    )
    wload = [
        pltpu.make_async_copy(w_ref.at[pl.ds(i * 1024, 1024)], wbuf.at[pl.ds(i * 1024, 1024)], ws.at[i])
        for i in range(4)
    ]
    start(wload)
    for c in load[9:]:
        c.wait()

    for i in range(16):
        ocos[i] = jnp.broadcast_to(hcos[i : i + 1, :], (128, 128)).T
        osin[i] = jnp.broadcast_to(hsin[i : i + 1, :], (128, 128)).T
    live_col[...] = jnp.broadcast_to(kbuf[z, SLOTS : SLOTS + 16, :][0:1].astype(F32), (128, 128)).T

    lane = lax.broadcasted_iota(jnp.int32, (128, 128), 1)
    row = lax.broadcasted_iota(jnp.int32, (SLOTS, HEAD_WIDTH), 0)

    def prepare(shards, kkt, count=3, first=0):
        for n, zz in enumerate(shards, first):
            slots = slice(n * SLOTS, (n + 1) * SLOTS)
            rubric = slice(count * SLOTS + n * RUB, count * SLOTS + (n + 1) * RUB)
            place = lax.div(zz, 4) * SLOTS
            rows = pl.ds(pl.multiple_of(place, SLOTS), SLOTS)
            length = lens[pl.ds(lax.rem(zz, 4), 1), :]
            kjt[:, slots] = turn(kbuf[zz, 0:SLOTS, :].astype(F32), jcos[rows, :], jsin[rows, :]).T
            kkt[:, rubric] = kbuf[zz, SLOTS:SHARD, :].astype(F32).T.astype(BF16)
            alive = row + place < length
            vaug[slots, 0:128] = jnp.where(alive, vbuf[zz, 0:SLOTS, :].astype(F32), 0.0).astype(BF16)
            vaug[slots, 128:256] = jnp.where(alive, 1.0, 0.0).astype(BF16)
            vaug[rubric, 0:128] = vbuf[zz, SLOTS:SHARD, :]
            vaug[rubric, 128:256] = jnp.ones((RUB, 128), BF16)

    def rotate(shards, slot, kkt):
        for n, zz in enumerate(shards):
            length = lens[pl.ds(lax.rem(zz, 4), 1), :]
            place = lax.div(zz, 4) * SLOTS
            co, so = ocos[slot * 4 + lax.rem(zz, 4)], osin[slot * 4 + lax.rem(zz, 4)]
            for i in range(SLOTS // 128):
                cols = slice(n * SLOTS + i * 128, n * SLOTS + (i + 1) * 128)
                k = kjt[:, cols]
                k = k * co + jnp.concatenate([k[64:], k[:64]], axis=0) * so
                alive = lane + (place + i * 128) < length
                kkt[:, cols] = jnp.where(alive, k, live_col[...]).astype(BF16)

    def share_rubric(n):
        kkt[n, :, 3 * SLOTS : 3 * SHARD] = kkt[0, :, 3 * SLOTS : 3 * SHARD]

    def flash(slot, keys, kkt, first=False, tiles=range(4)):
        scores = [
            jnp.dot(qbuf[slot, i * 256 : (i + 1) * 256, :], kkt[:, 0:keys], preferred_element_type=F32)
            for i in tiles
        ]
        for s, i in zip(scores, tiles):
            rows = slice(i * 256, (i + 1) * 256)
            top = jnp.max(s, axis=1, keepdims=True) * SCALE
            if first:
                new = jnp.broadcast_to(top, (256, 128))
            else:
                old = peak[slot, rows, :]
                new = jnp.maximum(old, top)
            p = jnp.exp2(s * SCALE - new[:, 0:1]).astype(BF16)
            o = jnp.dot(p, vaug[0:keys, :], preferred_element_type=F32)
            if first:
                acc[slot, rows, :] = o
            else:
                f = jnp.exp2(old - new)
                acc[slot, rows, 0:128] = acc[slot, rows, 0:128] * f + o[:, 0:128]
                acc[slot, rows, 128:256] = acc[slot, rows, 128:256] * f + o[:, 128:256]
            peak[slot, rows, :] = new

    near = (z, zs(-1), zs(1))

    def ordered(n, base):
        return lax.rem(y + base + 3 * n + 3 * lax.div(n, 2) + 2 * lax.div(n, 3), 4)

    one = kkt.at[0]
    prepare(near[:1], one)
    forward(0, 1)
    arrived(qdir)
    start(qfwd)
    forward(0, 0)
    prepare(near[1:], one, 3, 1)

    def unit_near(n, carry):
        slot = ordered(n, 0)

        @pl.when(n == 2)
        def _():
            forward(1, 1)

        @pl.when(n == 3)
        def _():
            forward(1, 0)
            arrived(qfwd)

        rotate(near, slot, one)
        flash(slot, 3 * SHARD, one, True)
        return carry

    lax.fori_loop(0, 4, unit_near, 0)

    forward(2, 1)
    second = (zs(-2), zs(2))
    prepare(second, one, 2)

    def unit_second(n, carry):
        slot = lax.rem(y + n, 4)

        @pl.when(n == 2)
        def _():
            forward(2, 0)

        rotate(second, slot, one)
        flash(slot, 2 * SHARD, one)
        return carry

    lax.fori_loop(0, 4, unit_second, 0)

    eye = lax.broadcasted_iota(jnp.int32, (CHUNK, 128), 0) == lax.broadcasted_iota(jnp.int32, (CHUNK, 128), 1)

    def outgoing(i, n, dev):
        return (
            copy(osend.at[i, n], obuf.at[i, n], os.at[i, n], orr.at[i, n], dev),
            copy(lsend.at[i, n], lbuf.at[i, n], ls.at[i, n], lr.at[i, n], dev),
        )

    def finish(i, n, slot):
        for h in range(GROUP):
            rows = slice(i * HALF + h * CHUNK, i * HALF + (h + 1) * CHUNK)
            total = acc[slot, rows, 128:256]
            stat = peak[slot, rows, :] + jnp.log2(total)
            osend[i, n, h * CHUNK : (h + 1) * CHUNK, :] = (acc[slot, rows, 0:128] / total).astype(BF16)
            lsend[i, n, h : h + 1, :] = jnp.sum(jnp.where(eye, stat, 0.0), axis=0, keepdims=True)

        @pl.when(n != 3)
        def _():
            start(outgoing(i, n, at(slot, z)))

    def last_slot(n):
        return ordered(n, 2)

    partials = [
        [outgoing(i, 0, beyond), outgoing(i, 1, north), outgoing(i, 2, south)] for i in range(2)
    ]

    def combine(i):
        for pair in partials[i]:
            arrived(pair)
        stats = [lbuf[i, 0], lbuf[i, 1], lbuf[i, 2], lsend[i, 3]]
        top = functools.reduce(jnp.maximum, stats)
        parts = [jnp.exp2(s - top) for s in stats]
        total = parts[0] + parts[1] + parts[2] + parts[3]
        shares = [jnp.concatenate([p / total] * 16, axis=0).T for p in parts]
        for h in range(GROUP):
            rows = slice(h * CHUNK, (h + 1) * CHUNK)
            out = None
            for n in range(4):
                src = osend[i, 3, rows, :] if n == 3 else obuf[i, n, rows, :]
                term = shares[n][0:CHUNK, h : h + 1] * src.astype(F32)
                out = term if out is None else out + term
            att[i, :, h * 128 : (h + 1) * 128] = out.astype(BF16)

    half = lax.div(head, 4)
    mine = half == rep
    u = lax.rem(x - 2 * rep + 8, 4)
    g = lax.rem(head, 4)
    far = 1 - rep

    swaps = [
        copy(att.at[i], fbuf.at[g, rep, i], zsend.at[i], zrecv.at[i], partner)
        for i in range(2)
    ]
    swapped = [
        copy(fbuf.at[g, far, i], fbuf.at[g, far, i], zsend.at[i], zrecv.at[i], partner)
        for i in range(2)
    ]

    def block(k, n):
        return fbuf.at[k, rep if n < 2 else far, n % 2]

    def hop(blk, n, way):
        return copy(blk, blk, xs.at[n, way], xr.at[n, way], (east, west)[way])

    def cross(blk, n, way):
        return copy(blk, blk, ds.at[n, way], dr.at[n, way], other)

    def spread(n):
        blk = block(g, n)
        start((hop(blk, n, 0), hop(blk, n, 1), cross(blk, n, 0)))

    def publish(i):
        combine(i)

        @pl.when(mine)
        def _():
            fbuf[g, rep, i] = att[i]
            spread(i)

        @pl.when(jnp.logical_not(mine))
        def _():
            swaps[i].start()

    low, high = core, 2 + core
    roles = ((low, high), (high, low), (high, low), (low, high))

    def collect(n):
        for which, (k0, k1) in enumerate(roles):

            @pl.when(u == which)
            def _():
                if which < 2:
                    blk = block(k1, n)
                    hop(blk, n, 1 - which).wait_recv()
                    cross(blk, n, 1).start()
                else:
                    way = which - 2
                    blk, blk1 = block(k0, n), block(k1, n)
                    hop(blk, n, way).wait_recv()
                    start((copy(blk, blk, fs.at[n], fr.at[n], (east, west)[way]), cross(blk, n, 0)))
                    copy(blk1, blk1, fs.at[n], fr.at[n], (east, west)[way]).wait_recv()
                    cross(blk1, n, 1).start()

    def crossed(n):
        blk = block(g, n)
        cross(blk, n, 0).wait_recv()
        cross(blk, n, 1).wait_recv()

    def product(r, i):
        total = None
        for k in range(4):
            term = jnp.dot(
                fbuf[k, r, i], wbuf[k * 1024 : (k + 1) * 1024, :], preferred_element_type=F32
            )
            total = term if total is None else total + term
        return total

    arrived(rings[3][0])
    arrived(rings[3][1])
    last = (zs(-3), zs(3), zs(4))
    for n in range(4):
        prepare(last, kkt.at[n], 3) if n == 0 else share_rubric(n)

    def unit_last(n, carry):
        slot = last_slot(n)
        rotate(last, slot, kkt.at[n])
        flash(slot, 3 * SHARD, kkt.at[n], tiles=(0, 1))
        finish(0, n, slot)
        return carry

    lax.fori_loop(0, 4, unit_last, 0)

    def unit_end(n, carry):
        slot = last_slot(n)

        @pl.when(n == 2)
        def _():
            publish(0)

        flash(slot, 3 * SHARD, kkt.at[n], tiles=(2, 3))
        finish(1, n, slot)
        return carry

    lax.fori_loop(0, 4, unit_end, 0)
    collect(0)
    publish(1)
    collect(1)
    for c in wload:
        c.wait()
    sends = []
    for i in range(2):

        @pl.when(mine)
        def _():
            swapped[i].wait_recv()
            spread(2 + i)

        collect(2 + i)
        crossed(2 + i)
        part[i] = product(far, i).astype(BF16)
        c = copy(part.at[i], got.at[i], ps.at[i], pr.at[i], partner)
        c.start()
        sends.append(c)
    crossed(0)
    crossed(1)
    own = [product(rep, i) for i in range(2)]
    for i in range(2):
        rows = slice(i * CHUNK, (i + 1) * CHUNK)
        sends[i].wait_recv()
        out_ref[rows, :] = (own[i] + got[i].astype(F32)).astype(BF16)

    for pairs in (*rings, (qdir, qfwd), *partials, (sends,)):
        for pair in pairs:
            for c in pair:
                c.wait_send()
    for n in range(4):
        blk = block(g, n)
        cross(blk, n, 0).wait_send()
        cross(blk, n, 1).wait_send()

    @pl.when(mine)
    def _():
        for n in range(4):
            hop(block(g, n), n, 0).wait_send()
            hop(block(g, n), n, 1).wait_send()

    @pl.when(jnp.logical_not(mine))
    def _():
        for n in range(4):
            blk = block(g, n)
            copy(blk, blk, fs.at[n], fr.at[n], east).wait_send()
        for c in swaps:
            c.wait_send()


VMEM = pl.BlockSpec(memory_space=pltpu.VMEM)
ANY = pl.BlockSpec(memory_space=pl.ANY)
DMA = pltpu.SemaphoreType.DMA


def local(
    queries, criteria_keys, criteria_values, candidate_keys, candidate_values,
    lengths, orders, out_weight,
):
    seg = lax.axis_index("seg")
    y, zl = lax.rem(seg, 4), lax.div(seg, 4)
    ids = jnp.arange(16, dtype=jnp.int32)
    views = lax.dynamic_slice_in_dim(orders, zl * 4, 4, 0)
    placed = views[:, :, None] == ids[None, None, :]
    placed_len = jnp.sum(jnp.where(placed, lengths[None, None, :], 0), axis=2)
    before = ids[None, :] < ids[:, None]
    starts = RUBRIC_LENGTH + jnp.sum(jnp.where(before[None], placed_len[:, None, :], 0), axis=2)
    offsets = jnp.sum(jnp.where(placed, starts[:, :, None], 0), axis=1)
    wanted = jnp.arange(4, dtype=jnp.int32) * 4 + y
    pick = wanted[:, None] == ids[None, :]
    offsets = jnp.sum(jnp.where(pick[None], offsets[:, None, :], 0), axis=2)
    mine = jnp.sum(jnp.where(pick, lengths[None, :], 0), axis=1)
    mine = jnp.broadcast_to(mine[:, None], (4, 128))
    hcos, hsin = tables(offsets.reshape(16))
    cos, sin = angle_tables()
    V = pltpu.VMEM
    return pl.pallas_call(
        fused_kernel,
        out_shape=jax.ShapeDtypeStruct((ROWS, 1024), BF16),
        in_specs=[ANY] * 11,
        out_specs=VMEM,
        scratch_shapes=[
            V((4, 128), jnp.int32), V((ROWS, 1024), BF16), V((SLOTS, 128), BF16), V((RUB, 128), BF16), V((SLOTS, 128), BF16),
            V((RUB, 128), BF16), V((1024, 128), F32), V((1024, 128), F32),
            V((16, 128), F32), V((16, 128), F32), V((128, 128), F32), V((128, 128), F32), V((128, 128), F32), V((128, 128), F32),
            V((16, 128, 128), F32), V((16, 128, 128), F32),
            V((4, 1024, 128), BF16), V((8, SHARD, 128), BF16), V((8, SHARD, 128), BF16),
            V((128, 3 * SLOTS), F32), V((4, 128, 3 * SHARD), BF16), V((3 * SHARD, 256), BF16), V((128, 128), F32),
            V((4, 1024, 256), F32), V((4, 1024, 128), F32),
            V((2, 4, HALF, 128), BF16), V((2, 4, 8, 128), F32),
            V((2, 4, HALF, 128), BF16), V((2, 4, 8, 128), F32),
            V((4096, 1024), BF16), V((4, 2, 2, CHUNK, 1024), BF16),
            V((2, CHUNK, 1024), BF16), V((2, CHUNK, 1024), BF16), V((2, CHUNK, 1024), BF16),
            DMA((14,)), DMA((4,)),
            DMA((4,)), DMA((4,)),
            DMA((2, 8)), DMA((2, 8)),
            DMA((2, 4)), DMA((2, 4)),
            DMA((2, 4)), DMA((2, 4)),
            DMA((2,)), DMA((2,)),
            DMA((4, 2)), DMA((4, 2)),
            DMA((4,)), DMA((4,)),
            DMA((4, 2)), DMA((4, 2)),
            DMA((2,)), DMA((2,)),
        ],
        compiler_params=pltpu.CompilerParams(
            collective_id=0, has_side_effects=True, vmem_limit_bytes=58 * 1024 * 1024
        ),
        name="judge",
    )(
        queries, criteria_keys, criteria_values, candidate_keys, candidate_values,
        jnp.asarray(cos), jnp.asarray(sin), out_weight, mine, hcos, hsin,
    )


def solution(mesh):
    rows = P(("seg", "rep"), "head")
    return jax.shard_map(
        local,
        mesh=mesh,
        in_specs=(rows, rows, rows, rows, rows, P(), P(), P("rep", "head")),
        out_specs=rows,
        check_vma=False,
    )
```

```python
import functools
import math

import jax
import jax.numpy as jnp
import numpy as np
from jax import lax
from jax.experimental import pallas as pl
from jax.experimental.pallas import tpu as pltpu
from jax.sharding import PartitionSpec as P

QUERY_HEADS = 64
KEY_VALUE_HEADS = 8
HEAD_WIDTH = 128
ANSWER_LENGTH = 1024
RUBRIC_LENGTH = 4096
THETA = 1000000.0
GROUP = 8
ROWS = 128
SLOTS = 512
RUB = 128
CHUNK = 64
LIVE_TOTAL = 10240
QUERY_START = RUBRIC_LENGTH + LIVE_TOTAL
SHARD = SLOTS + RUB
HALF = GROUP * CHUNK
SCALE = math.log2(math.e) / math.sqrt(HEAD_WIDTH)
MESH = pl.DeviceIdType.MESH
F32 = jnp.float32
BF16 = jnp.bfloat16


def angle_tables():
    halfway = HEAD_WIDTH // 2
    exponent = np.arange(halfway, dtype=np.float32) * np.float32(-2.0 * math.log(THETA) / HEAD_WIDTH)
    frequency = np.exp(exponent).astype(np.float32)
    positions = np.concatenate([
        np.arange(RUBRIC_LENGTH), QUERY_START + np.arange(2 * ROWS), 128 * np.arange(128),
    ]).astype(np.float32)
    angles = (positions[:, None] * frequency[None, :]).astype(np.float64)
    cos, sin = np.cos(angles), np.sin(angles)
    return (
        np.concatenate([cos, cos], axis=1).astype(np.float32),
        np.concatenate([-sin, sin], axis=1).astype(np.float32),
    )


def turn(x, cos, sin):
    return x * cos + pltpu.roll(x, HEAD_WIDTH // 2, 1) * sin


def fused_kernel(
    q_ref, rk_ref, rv_ref, ck_ref, cv_ref, cos_ref, sin_ref, w_ref, len_ref, order_ref,
    out_ref,
    len_in, order_in, lens, offs, qin, cvin, rvin, ckin, rkin, jcos, jsin, hcos, hsin, qcos, qsin, rcos, rsin, ocos, osin,
    qbuf, kbuf, vbuf, kjt, kkt, vaug, live_col, acc, peak, obuf, lbuf, osend, lsend,
    wbuf, fbuf, att, part, got,
    ins, ws, qs, qr, cs, cr, os, orr, ls, lr,
    zsend, zrecv, xs, xr, fs, fr, ds, dr, ps, pr,
):
    seg = lax.axis_index("seg")
    rep = lax.axis_index("rep")
    head = lax.axis_index("head")
    y = lax.rem(seg, 4)
    zl = lax.div(seg, 4)
    z = rep * 4 + zl
    x = lax.div(head, 2)
    core = lax.rem(head, 2)

    def at(yy, zz):
        yy = lax.rem(yy + 8, 4)
        zz = lax.rem(zz + 16, 8)
        return {"seg": lax.rem(zz, 4) * 4 + yy, "rep": lax.div(zz, 4)}

    def zs(d):
        return lax.rem(z + d + 16, 8)

    def ys(d):
        return lax.rem(y + d + 8, 4)

    def copy(src, dst, ssem, rsem, dev):
        return pltpu.make_async_remote_copy(
            src_ref=src, dst_ref=dst, send_sem=ssem, recv_sem=rsem,
            device_id=dev, device_id_type=MESH,
        )

    def start(pair):
        for c in pair:
            c.start()

    def arrived(pair):
        for c in pair:
            c.wait_recv()

    mine_rows = pl.ds((seg * 2 + rep) * RUB, RUB)
    query_rows = pl.ds(RUBRIC_LENGTH + rep * ROWS, ROWS)
    high_rows = pl.ds(RUBRIC_LENGTH + 2 * ROWS, 128)
    low_rows = pl.ds(0, 1024)
    load = [
        pltpu.make_async_copy(a, b, ins.at[i])
        for i, (a, b) in enumerate((
            (cv_ref, cvin), (rv_ref, rvin),
            (q_ref, qin), (cos_ref.at[query_rows], qcos), (sin_ref.at[query_rows], qsin),
            (ck_ref, ckin), (rk_ref, rkin),
            (cos_ref.at[mine_rows], rcos), (sin_ref.at[mine_rows], rsin),
            (cos_ref.at[high_rows], hcos), (sin_ref.at[high_rows], hsin),
            (len_ref, len_in), (order_ref, order_in),
            (cos_ref.at[low_rows], jcos), (sin_ref.at[low_rows], jsin),
        ))
    ]
    start(load)

    up, down = at(y, z + 1), at(y, z - 1)
    north, south, beyond = at(y + 1, z), at(y - 1, z), at(y + 2, z)
    east = {"head": lax.rem(x + 1, 4) * 2 + core}
    west = {"head": lax.rem(x + 3, 4) * 2 + core}
    other = {"head": x * 2 + 1 - core}
    partner = {"rep": 1 - rep}
    barrier = pltpu.get_barrier_semaphore()
    peers = (up, down, north, south, beyond, east, west, other, partner)
    for dev in peers:
        pl.semaphore_signal(barrier, inc=1, device_id=dev, device_id_type=MESH)
    pl.semaphore_wait(barrier, len(peers))

    def ring(step, c):
        a, b = zs(-step), zs(step)
        buf = (kbuf, vbuf)[c]
        ahead = copy(buf.at[a], buf.at[a], cs.at[0, step * 2 + c], cr.at[0, step * 2 + c], up)
        back = copy(buf.at[b], buf.at[b], cs.at[1, step * 2 + c], cr.at[1, step * 2 + c], down)
        if step < 3:
            return (ahead, back)
        return (ahead,) if c == 1 else (back,)

    rings = [[ring(s, c) for c in range(2)] for s in range(4)]

    def forward(step, c):
        arrived(rings[step][c])
        start(rings[step + 1][c])

    for c in load[:2]:
        c.wait()
    vbuf[z, 0:SLOTS, :] = cvin[...]
    vbuf[z, SLOTS:SHARD, :] = rvin[...]
    start(rings[0][1])
    for c in load[2:5]:
        c.wait()
    cq, sq = qcos[...], qsin[...]
    for h in range(GROUP):
        v = turn(qin[:, h * 128 : (h + 1) * 128].astype(F32), cq, sq).astype(BF16)
        qbuf[y, h * CHUNK : (h + 1) * CHUNK, :] = v[:CHUNK]
        qbuf[y, HALF + h * CHUNK : HALF + (h + 1) * CHUNK, :] = v[CHUNK:]
    qdir = (
        copy(qbuf.at[y], qbuf.at[y], qs.at[0], qr.at[0], north),
        copy(qbuf.at[y], qbuf.at[y], qs.at[1], qr.at[1], south),
    )
    start(qdir)
    for c in load[5:9]:
        c.wait()
    kbuf[z, 0:SLOTS, :] = ckin[...]
    kbuf[z, SLOTS:SHARD, :] = turn(rkin[...].astype(F32), rcos[...], rsin[...]).astype(BF16)
    start(rings[0][0])
    south_slot, north_slot = ys(-1), ys(1)
    qfwd = (
        copy(qbuf.at[south_slot, 0:HALF], qbuf.at[south_slot, 0:HALF], qs.at[2], qr.at[2], north),
        copy(qbuf.at[north_slot, HALF:], qbuf.at[north_slot, HALF:], qs.at[3], qr.at[3], south),
    )
    wload = [
        pltpu.make_async_copy(w_ref.at[pl.ds(i * 1024, 1024)], wbuf.at[pl.ds(i * 1024, 1024)], ws.at[i])
        for i in range(4)
    ]
    start(wload)
    for c in load[9:]:
        c.wait()

    place_row = lax.broadcasted_iota(jnp.int32, (128, 128), 0)

    def row_of(table, index):
        return jnp.sum(jnp.where(place_row == index, table[0:128, :], 0.0), axis=0, keepdims=True)

    first = lax.broadcasted_iota(jnp.int32, (16, 16), 0)
    second_index = lax.broadcasted_iota(jnp.int32, (16, 16), 1)
    same = first == second_index

    def column(values):
        return jnp.sum(jnp.where(same, values, 0.0), axis=1, keepdims=True)

    len_col = column(len_in[...].astype(F32))
    lens[...] = jnp.broadcast_to(len_col, (16, 128)).astype(jnp.int32)
    for a in range(4):
        placed = first == order_in[pl.ds(zl * 4 + a, 1), :]
        placed_len = jnp.sum(jnp.where(placed, len_col, 0.0), axis=0, keepdims=True)
        before = jnp.sum(jnp.where(first < second_index, column(placed_len), 0.0), axis=0, keepdims=True)
        offset = RUBRIC_LENGTH + jnp.sum(jnp.where(placed, before, 0.0), axis=1, keepdims=True)
        offs[a] = jnp.broadcast_to(offset, (16, 128)).astype(jnp.int32)
    for i in range(16):
        offset = offs[i // 4, pl.ds(i % 4 * 4 + y, 1), :]
        hi, lo = lax.shift_right_logical(offset, 7), lax.bitwise_and(offset, 127)
        ch, sh = row_of(hcos, hi), row_of(hsin, hi)
        cl, sl = row_of(jcos, lo), row_of(jsin, lo)
        ocos[i] = jnp.broadcast_to(ch * cl - sh * sl, (128, 128)).T
        osin[i] = jnp.broadcast_to(sh * cl + ch * sl, (128, 128)).T
    live_col[...] = jnp.broadcast_to(kbuf[z, SLOTS : SLOTS + 16, :][0:1].astype(F32), (128, 128)).T

    lane = lax.broadcasted_iota(jnp.int32, (128, 128), 1)
    row = lax.broadcasted_iota(jnp.int32, (SLOTS, HEAD_WIDTH), 0)

    def prepare(shards, kkt, count=3, first=0):
        for n, zz in enumerate(shards, first):
            slots = slice(n * SLOTS, (n + 1) * SLOTS)
            rubric = slice(count * SLOTS + n * RUB, count * SLOTS + (n + 1) * RUB)
            place = lax.div(zz, 4) * SLOTS
            rows = pl.ds(pl.multiple_of(place, SLOTS), SLOTS)
            length = lens[pl.ds(lax.rem(zz, 4) * 4 + y, 1), :]
            kjt[:, slots] = turn(kbuf[zz, 0:SLOTS, :].astype(F32), jcos[rows, :], jsin[rows, :]).T
            kkt[:, rubric] = kbuf[zz, SLOTS:SHARD, :].astype(F32).T.astype(BF16)
            alive = row + place < length
            vaug[slots, 0:128] = jnp.where(alive, vbuf[zz, 0:SLOTS, :].astype(F32), 0.0).astype(BF16)
            vaug[slots, 128:256] = jnp.where(alive, 1.0, 0.0).astype(BF16)
            vaug[rubric, 0:128] = vbuf[zz, SLOTS:SHARD, :]
            vaug[rubric, 128:256] = jnp.ones((RUB, 128), BF16)

    def rotate(shards, slot, kkt):
        for n, zz in enumerate(shards):
            length = lens[pl.ds(lax.rem(zz, 4) * 4 + y, 1), :]
            place = lax.div(zz, 4) * SLOTS
            co, so = ocos[slot * 4 + lax.rem(zz, 4)], osin[slot * 4 + lax.rem(zz, 4)]
            for i in range(SLOTS // 128):
                cols = slice(n * SLOTS + i * 128, n * SLOTS + (i + 1) * 128)
                k = kjt[:, cols]
                k = k * co + jnp.concatenate([k[64:], k[:64]], axis=0) * so
                alive = lane + (place + i * 128) < length
                kkt[:, cols] = jnp.where(alive, k, live_col[...]).astype(BF16)

    def share_rubric(n):
        kkt[n, :, 3 * SLOTS : 3 * SHARD] = kkt[0, :, 3 * SLOTS : 3 * SHARD]

    def flash(slot, keys, kkt, first=False, tiles=range(4)):
        scores = [
            jnp.dot(qbuf[slot, i * 256 : (i + 1) * 256, :], kkt[:, 0:keys], preferred_element_type=F32)
            for i in tiles
        ]
        for s, i in zip(scores, tiles):
            rows = slice(i * 256, (i + 1) * 256)
            top = jnp.max(s, axis=1, keepdims=True) * SCALE
            if first:
                new = jnp.broadcast_to(top, (256, 128))
            else:
                old = peak[slot, rows, :]
                new = jnp.maximum(old, top)
            p = jnp.exp2(s * SCALE - new[:, 0:1]).astype(BF16)
            o = jnp.dot(p, vaug[0:keys, :], preferred_element_type=F32)
            if first:
                acc[slot, rows, :] = o
            else:
                f = jnp.exp2(old - new)
                acc[slot, rows, 0:128] = acc[slot, rows, 0:128] * f + o[:, 0:128]
                acc[slot, rows, 128:256] = acc[slot, rows, 128:256] * f + o[:, 128:256]
            peak[slot, rows, :] = new

    near = (z, zs(-1), zs(1))

    def ordered(n, base):
        return lax.rem(y + base + 3 * n + 3 * lax.div(n, 2) + 2 * lax.div(n, 3), 4)

    one = kkt.at[0]
    prepare(near[:1], one)
    forward(0, 1)
    arrived(qdir)
    start(qfwd)
    forward(0, 0)
    prepare(near[1:], one, 3, 1)

    def unit_near(n, carry):
        slot = ordered(n, 0)

        @pl.when(n == 2)
        def _():
            forward(1, 1)

        @pl.when(n == 3)
        def _():
            forward(1, 0)
            arrived(qfwd)

        rotate(near, slot, one)
        flash(slot, 3 * SHARD, one, True)
        return carry

    lax.fori_loop(0, 4, unit_near, 0)

    forward(2, 1)
    second = (zs(-2), zs(2))
    prepare(second, one, 2)

    def unit_second(n, carry):
        slot = lax.rem(y + n, 4)

        @pl.when(n == 2)
        def _():
            forward(2, 0)

        rotate(second, slot, one)
        flash(slot, 2 * SHARD, one)
        return carry

    lax.fori_loop(0, 4, unit_second, 0)

    eye = lax.broadcasted_iota(jnp.int32, (CHUNK, 128), 0) == lax.broadcasted_iota(jnp.int32, (CHUNK, 128), 1)

    def outgoing(i, n, dev):
        return (
            copy(osend.at[i, n], obuf.at[i, n], os.at[i, n], orr.at[i, n], dev),
            copy(lsend.at[i, n], lbuf.at[i, n], ls.at[i, n], lr.at[i, n], dev),
        )

    def finish(i, n, slot):
        for h in range(GROUP):
            rows = slice(i * HALF + h * CHUNK, i * HALF + (h + 1) * CHUNK)
            total = acc[slot, rows, 128:256]
            stat = peak[slot, rows, :] + jnp.log2(total)
            osend[i, n, h * CHUNK : (h + 1) * CHUNK, :] = (acc[slot, rows, 0:128] / total).astype(BF16)
            lsend[i, n, h : h + 1, :] = jnp.sum(jnp.where(eye, stat, 0.0), axis=0, keepdims=True)

        @pl.when(n != 3)
        def _():
            start(outgoing(i, n, at(slot, z)))

    def last_slot(n):
        return ordered(n, 2)

    partials = [
        [outgoing(i, 0, beyond), outgoing(i, 1, north), outgoing(i, 2, south)] for i in range(2)
    ]

    def combine(i):
        for pair in partials[i]:
            arrived(pair)
        stats = [lbuf[i, 0], lbuf[i, 1], lbuf[i, 2], lsend[i, 3]]
        top = functools.reduce(jnp.maximum, stats)
        parts = [jnp.exp2(s - top) for s in stats]
        total = parts[0] + parts[1] + parts[2] + parts[3]
        shares = [jnp.concatenate([p / total] * 16, axis=0).T for p in parts]
        for h in range(GROUP):
            rows = slice(h * CHUNK, (h + 1) * CHUNK)
            out = None
            for n in range(4):
                src = osend[i, 3, rows, :] if n == 3 else obuf[i, n, rows, :]
                term = shares[n][0:CHUNK, h : h + 1] * src.astype(F32)
                out = term if out is None else out + term
            att[i, :, h * 128 : (h + 1) * 128] = out.astype(BF16)

    half = lax.div(head, 4)
    mine = half == rep
    u = lax.rem(x - 2 * rep + 8, 4)
    g = lax.rem(head, 4)
    far = 1 - rep

    swaps = [
        copy(att.at[i], fbuf.at[g, rep, i], zsend.at[i], zrecv.at[i], partner)
        for i in range(2)
    ]
    swapped = [
        copy(fbuf.at[g, far, i], fbuf.at[g, far, i], zsend.at[i], zrecv.at[i], partner)
        for i in range(2)
    ]

    def block(k, n):
        return fbuf.at[k, rep if n < 2 else far, n % 2]

    def hop(blk, n, way):
        return copy(blk, blk, xs.at[n, way], xr.at[n, way], (east, west)[way])

    def cross(blk, n, way):
        return copy(blk, blk, ds.at[n, way], dr.at[n, way], other)

    def spread(n):
        blk = block(g, n)
        start((hop(blk, n, 0), hop(blk, n, 1), cross(blk, n, 0)))

    def publish(i):
        combine(i)

        @pl.when(mine)
        def _():
            fbuf[g, rep, i] = att[i]
            spread(i)

        @pl.when(jnp.logical_not(mine))
        def _():
            swaps[i].start()

    low, high = core, 2 + core
    roles = ((low, high), (high, low), (high, low), (low, high))

    def collect(n):
        for which, (k0, k1) in enumerate(roles):

            @pl.when(u == which)
            def _():
                if which < 2:
                    blk = block(k1, n)
                    hop(blk, n, 1 - which).wait_recv()
                    cross(blk, n, 1).start()
                else:
                    way = which - 2
                    blk, blk1 = block(k0, n), block(k1, n)
                    hop(blk, n, way).wait_recv()
                    start((copy(blk, blk, fs.at[n], fr.at[n], (east, west)[way]), cross(blk, n, 0)))
                    copy(blk1, blk1, fs.at[n], fr.at[n], (east, west)[way]).wait_recv()
                    cross(blk1, n, 1).start()

    def crossed(n):
        blk = block(g, n)
        cross(blk, n, 0).wait_recv()
        cross(blk, n, 1).wait_recv()

    def product(r, i):
        total = None
        for k in range(4):
            term = jnp.dot(
                fbuf[k, r, i], wbuf[k * 1024 : (k + 1) * 1024, :], preferred_element_type=F32
            )
            total = term if total is None else total + term
        return total

    arrived(rings[3][0])
    arrived(rings[3][1])
    last = (zs(-3), zs(3), zs(4))
    for n in range(4):
        prepare(last, kkt.at[n], 3) if n == 0 else share_rubric(n)

    def unit_last(n, carry):
        slot = last_slot(n)
        rotate(last, slot, kkt.at[n])
        flash(slot, 3 * SHARD, kkt.at[n], tiles=(0, 1))
        finish(0, n, slot)
        return carry

    lax.fori_loop(0, 4, unit_last, 0)

    def unit_end(n, carry):
        slot = last_slot(n)

        @pl.when(n == 2)
        def _():
            publish(0)

        flash(slot, 3 * SHARD, kkt.at[n], tiles=(2, 3))
        finish(1, n, slot)
        return carry

    lax.fori_loop(0, 4, unit_end, 0)
    collect(0)
    publish(1)
    collect(1)
    for c in wload:
        c.wait()
    sends = []
    for i in range(2):

        @pl.when(mine)
        def _():
            swapped[i].wait_recv()
            spread(2 + i)

        collect(2 + i)
        crossed(2 + i)
        part[i] = product(far, i).astype(BF16)
        c = copy(part.at[i], got.at[i], ps.at[i], pr.at[i], partner)
        c.start()
        sends.append(c)
    crossed(0)
    crossed(1)
    own = [product(rep, i) for i in range(2)]
    for i in range(2):
        rows = slice(i * CHUNK, (i + 1) * CHUNK)
        sends[i].wait_recv()
        out_ref[rows, :] = (own[i] + got[i].astype(F32)).astype(BF16)

    for pairs in (*rings, (qdir, qfwd), *partials, (sends,)):
        for pair in pairs:
            for c in pair:
                c.wait_send()
    for n in range(4):
        blk = block(g, n)
        cross(blk, n, 0).wait_send()
        cross(blk, n, 1).wait_send()

    @pl.when(mine)
    def _():
        for n in range(4):
            hop(block(g, n), n, 0).wait_send()
            hop(block(g, n), n, 1).wait_send()

    @pl.when(jnp.logical_not(mine))
    def _():
        for n in range(4):
            blk = block(g, n)
            copy(blk, blk, fs.at[n], fr.at[n], east).wait_send()
        for c in swaps:
            c.wait_send()


VMEM = pl.BlockSpec(memory_space=pltpu.VMEM)
ANY = pl.BlockSpec(memory_space=pl.ANY)
DMA = pltpu.SemaphoreType.DMA


def local(
    queries, criteria_keys, criteria_values, candidate_keys, candidate_values,
    lengths, orders, out_weight,
):
    cos, sin = angle_tables()
    V = pltpu.VMEM
    return pl.pallas_call(
        fused_kernel,
        out_shape=jax.ShapeDtypeStruct((ROWS, 1024), BF16),
        in_specs=[ANY] * 10,
        out_specs=VMEM,
        scratch_shapes=[
            V((1, 16), jnp.int32), V((16, 16), jnp.int32), V((16, 128), jnp.int32), V((4, 16, 128), jnp.int32),
            V((ROWS, 1024), BF16), V((SLOTS, 128), BF16), V((RUB, 128), BF16), V((SLOTS, 128), BF16),
            V((RUB, 128), BF16), V((1024, 128), F32), V((1024, 128), F32),
            V((128, 128), F32), V((128, 128), F32), V((128, 128), F32), V((128, 128), F32), V((128, 128), F32), V((128, 128), F32),
            V((16, 128, 128), F32), V((16, 128, 128), F32),
            V((4, 1024, 128), BF16), V((8, SHARD, 128), BF16), V((8, SHARD, 128), BF16),
            V((128, 3 * SLOTS), F32), V((4, 128, 3 * SHARD), BF16), V((3 * SHARD, 256), BF16), V((128, 128), F32),
            V((4, 1024, 256), F32), V((4, 1024, 128), F32),
            V((2, 4, HALF, 128), BF16), V((2, 4, 8, 128), F32),
            V((2, 4, HALF, 128), BF16), V((2, 4, 8, 128), F32),
            V((4096, 1024), BF16), V((4, 2, 2, CHUNK, 1024), BF16),
            V((2, CHUNK, 1024), BF16), V((2, CHUNK, 1024), BF16), V((2, CHUNK, 1024), BF16),
            DMA((15,)), DMA((4,)),
            DMA((4,)), DMA((4,)),
            DMA((2, 8)), DMA((2, 8)),
            DMA((2, 4)), DMA((2, 4)),
            DMA((2, 4)), DMA((2, 4)),
            DMA((2,)), DMA((2,)),
            DMA((4, 2)), DMA((4, 2)),
            DMA((4,)), DMA((4,)),
            DMA((4, 2)), DMA((4, 2)),
            DMA((2,)), DMA((2,)),
        ],
        compiler_params=pltpu.CompilerParams(
            collective_id=0, has_side_effects=True, vmem_limit_bytes=58 * 1024 * 1024
        ),
        name="judge",
    )(
        queries, criteria_keys, criteria_values, candidate_keys, candidate_values,
        jnp.asarray(cos), jnp.asarray(sin), out_weight, lengths.reshape(1, 16), orders,
    )


def solution(mesh):
    rows = P(("seg", "rep"), "head")
    return jax.shard_map(
        local,
        mesh=mesh,
        in_specs=(rows, rows, rows, rows, rows, P(), P(), P("rep", "head")),
        out_specs=rows,
        check_vma=False,
    )
```

```python
import functools
import math

import jax
import jax.numpy as jnp
import numpy as np
from jax import lax
from jax.experimental import pallas as pl
from jax.experimental.pallas import tpu as pltpu
from jax.sharding import PartitionSpec as P

QUERY_HEADS = 64
KEY_VALUE_HEADS = 8
HEAD_WIDTH = 128
ANSWER_LENGTH = 1024
RUBRIC_LENGTH = 4096
THETA = 1000000.0
GROUP = 8
ROWS = 128
SLOTS = 512
RUB = 128
CHUNK = 64
LIVE_TOTAL = 10240
QUERY_START = RUBRIC_LENGTH + LIVE_TOTAL
SHARD = SLOTS + RUB
HALF = GROUP * CHUNK
SCALE = math.log2(math.e) / math.sqrt(HEAD_WIDTH)
MESH = pl.DeviceIdType.MESH
F32 = jnp.float32
BF16 = jnp.bfloat16


def angle_tables():
    halfway = HEAD_WIDTH // 2
    exponent = np.arange(halfway, dtype=np.float32) * np.float32(-2.0 * math.log(THETA) / HEAD_WIDTH)
    frequency = np.exp(exponent).astype(np.float32)
    positions = np.concatenate([
        np.arange(RUBRIC_LENGTH), QUERY_START + np.arange(2 * ROWS), 128 * np.arange(128),
    ]).astype(np.float32)
    angles = (positions[:, None] * frequency[None, :]).astype(np.float64)
    cos, sin = np.cos(angles), np.sin(angles)
    return (
        np.concatenate([cos, cos], axis=1).astype(np.float32),
        np.concatenate([-sin, sin], axis=1).astype(np.float32),
    )


def turn(x, cos, sin):
    return x * cos + pltpu.roll(x, HEAD_WIDTH // 2, 1) * sin


def fused_kernel(
    q_ref, rk_ref, rv_ref, ck_ref, cv_ref, cos_ref, sin_ref, w_ref, len_ref, order_ref,
    out_ref,
    len_in, order_in, lens, offs, qin, cvin, rvin, ckin, rkin, jcos, jsin, hcos, hsin, qcos, qsin, rcos, rsin, ocos, osin,
    qbuf, kbuf, vbuf, kjt, kkt, vaug, live_col, acc, peak, obuf, lbuf, osend, lsend,
    wbuf, fbuf, att, part, got,
    ins, ws, qs, qr, cs, cr, os, orr, ls, lr,
    zsend, zrecv, xs, xr, fs, fr, ds, dr, ps, pr,
):
    seg = lax.axis_index("seg")
    rep = lax.axis_index("rep")
    head = lax.axis_index("head")
    y = lax.rem(seg, 4)
    zl = lax.div(seg, 4)
    z = rep * 4 + zl
    x = lax.div(head, 2)
    core = lax.rem(head, 2)

    def at(yy, zz):
        yy = lax.rem(yy + 8, 4)
        zz = lax.rem(zz + 16, 8)
        return {"seg": lax.rem(zz, 4) * 4 + yy, "rep": lax.div(zz, 4)}

    def zs(d):
        return lax.rem(z + d + 16, 8)

    def ys(d):
        return lax.rem(y + d + 8, 4)

    def copy(src, dst, ssem, rsem, dev):
        return pltpu.make_async_remote_copy(
            src_ref=src, dst_ref=dst, send_sem=ssem, recv_sem=rsem,
            device_id=dev, device_id_type=MESH,
        )

    def start(pair):
        for c in pair:
            c.start()

    def arrived(pair):
        for c in pair:
            c.wait_recv()

    mine_rows = pl.ds((seg * 2 + rep) * RUB, RUB)
    query_rows = pl.ds(RUBRIC_LENGTH + rep * ROWS, ROWS)
    high_rows = pl.ds(RUBRIC_LENGTH + 2 * ROWS, 128)
    low_rows = pl.ds(0, 1024)
    load = [
        pltpu.make_async_copy(a, b, ins.at[i])
        for i, (a, b) in enumerate((
            (cv_ref, cvin), (rv_ref, rvin),
            (q_ref, qin), (cos_ref.at[query_rows], qcos), (sin_ref.at[query_rows], qsin),
            (ck_ref, ckin), (rk_ref, rkin),
            (cos_ref.at[mine_rows], rcos), (sin_ref.at[mine_rows], rsin),
            (cos_ref.at[high_rows], hcos), (sin_ref.at[high_rows], hsin),
            (len_ref, len_in), (order_ref, order_in),
            (cos_ref.at[low_rows], jcos), (sin_ref.at[low_rows], jsin),
        ))
    ]
    start(load)

    up, down = at(y, z + 1), at(y, z - 1)
    north, south, beyond = at(y + 1, z), at(y - 1, z), at(y + 2, z)
    east = {"head": lax.rem(x + 1, 4) * 2 + core}
    west = {"head": lax.rem(x + 3, 4) * 2 + core}
    other = {"head": x * 2 + 1 - core}
    partner = {"rep": 1 - rep}
    barrier = pltpu.get_barrier_semaphore()
    peers = (up, down, north, south, beyond, east, west, other, partner)
    for dev in peers:
        pl.semaphore_signal(barrier, inc=1, device_id=dev, device_id_type=MESH)
    pl.semaphore_wait(barrier, len(peers))

    def ring(step, c):
        a, b = zs(-step), zs(step)
        buf = (kbuf, vbuf)[c]
        ahead = copy(buf.at[a], buf.at[a], cs.at[0, step * 2 + c], cr.at[0, step * 2 + c], up)
        back = copy(buf.at[b], buf.at[b], cs.at[1, step * 2 + c], cr.at[1, step * 2 + c], down)
        if step < 3:
            return (ahead, back)
        return (ahead,) if c == 1 else (back,)

    rings = [[ring(s, c) for c in range(2)] for s in range(4)]

    def forward(step, c):
        arrived(rings[step][c])
        start(rings[step + 1][c])

    for c in load[:2]:
        c.wait()
    vbuf[z, 0:SLOTS, :] = cvin[...]
    vbuf[z, SLOTS:SHARD, :] = rvin[...]
    start(rings[0][1])
    for c in load[2:5]:
        c.wait()
    cq, sq = qcos[...], qsin[...]
    for h in range(GROUP):
        v = turn(qin[:, h * 128 : (h + 1) * 128].astype(F32), cq, sq).astype(BF16)
        qbuf[y, h * CHUNK : (h + 1) * CHUNK, :] = v[:CHUNK]
        qbuf[y, HALF + h * CHUNK : HALF + (h + 1) * CHUNK, :] = v[CHUNK:]
    qdir = (
        copy(qbuf.at[y], qbuf.at[y], qs.at[0], qr.at[0], north),
        copy(qbuf.at[y], qbuf.at[y], qs.at[1], qr.at[1], south),
    )
    start(qdir)
    for c in load[5:9]:
        c.wait()
    kbuf[z, 0:SLOTS, :] = ckin[...]
    kbuf[z, SLOTS:SHARD, :] = turn(rkin[...].astype(F32), rcos[...], rsin[...]).astype(BF16)
    start(rings[0][0])
    south_slot, north_slot = ys(-1), ys(1)
    qfwd = (
        copy(qbuf.at[south_slot, 0:HALF], qbuf.at[south_slot, 0:HALF], qs.at[2], qr.at[2], north),
        copy(qbuf.at[north_slot, HALF:], qbuf.at[north_slot, HALF:], qs.at[3], qr.at[3], south),
    )
    wload = [
        pltpu.make_async_copy(w_ref.at[pl.ds(i * 1024, 1024)], wbuf.at[pl.ds(i * 1024, 1024)], ws.at[i])
        for i in range(4)
    ]
    start(wload)
    for c in load[9:]:
        c.wait()

    place_row = lax.broadcasted_iota(jnp.int32, (128, 128), 0)

    def row_of(table, index):
        return jnp.sum(jnp.where(place_row == index, table[0:128, :], 0.0), axis=0, keepdims=True)

    first = lax.broadcasted_iota(jnp.int32, (16, 16), 0)
    second_index = lax.broadcasted_iota(jnp.int32, (16, 16), 1)
    same = first == second_index

    def column(values):
        return jnp.sum(jnp.where(same, values, 0.0), axis=1, keepdims=True)

    len_col = column(len_in[...].astype(F32))
    lens[...] = jnp.broadcast_to(len_col, (16, 128)).astype(jnp.int32)
    for a in range(4):
        placed = first == order_in[pl.ds(zl * 4 + a, 1), :]
        placed_len = jnp.sum(jnp.where(placed, len_col, 0.0), axis=0, keepdims=True)
        before = jnp.sum(jnp.where(first < second_index, column(placed_len), 0.0), axis=0, keepdims=True)
        offset = RUBRIC_LENGTH + jnp.sum(jnp.where(placed, before, 0.0), axis=1, keepdims=True)
        offs[a] = jnp.broadcast_to(offset, (16, 128)).astype(jnp.int32)
    for i in range(16):
        offset = offs[i // 4, pl.ds(i % 4 * 4 + y, 1), :]
        hi, lo = lax.shift_right_logical(offset, 7), lax.bitwise_and(offset, 127)
        ch, sh = row_of(hcos, hi), row_of(hsin, hi)
        cl, sl = row_of(jcos, lo), row_of(jsin, lo)
        ocos[i] = jnp.broadcast_to(ch * cl - sh * sl, (128, 128)).T
        osin[i] = jnp.broadcast_to(sh * cl + ch * sl, (128, 128)).T
    live_col[...] = jnp.broadcast_to(kbuf[z, SLOTS : SLOTS + 16, :][0:1].astype(F32), (128, 128)).T

    lane = lax.broadcasted_iota(jnp.int32, (128, 128), 1)
    row = lax.broadcasted_iota(jnp.int32, (SLOTS, HEAD_WIDTH), 0)

    def prepare(shards, kkt, count=3, first=0):
        for n, zz in enumerate(shards, first):
            slots = slice(n * SLOTS, (n + 1) * SLOTS)
            rubric = slice(count * SLOTS + n * RUB, count * SLOTS + (n + 1) * RUB)
            place = lax.div(zz, 4) * SLOTS
            rows = pl.ds(pl.multiple_of(place, SLOTS), SLOTS)
            length = lens[pl.ds(lax.rem(zz, 4) * 4 + y, 1), :]
            kjt[:, slots] = turn(kbuf[zz, 0:SLOTS, :].astype(F32), jcos[rows, :], jsin[rows, :]).T
            kkt[:, rubric] = kbuf[zz, SLOTS:SHARD, :].astype(F32).T.astype(BF16)
            alive = row + place < length
            vaug[slots, 0:128] = jnp.where(alive, vbuf[zz, 0:SLOTS, :].astype(F32), 0.0).astype(BF16)
            vaug[slots, 128:256] = jnp.where(alive, 1.0, 0.0).astype(BF16)
            vaug[rubric, 0:128] = vbuf[zz, SLOTS:SHARD, :]
            vaug[rubric, 128:256] = jnp.ones((RUB, 128), BF16)

    def rotate(shards, slot, kkt):
        for n, zz in enumerate(shards):
            length = lens[pl.ds(lax.rem(zz, 4) * 4 + y, 1), :]
            place = lax.div(zz, 4) * SLOTS
            co, so = ocos[slot * 4 + lax.rem(zz, 4)], osin[slot * 4 + lax.rem(zz, 4)]
            for i in range(SLOTS // 128):
                cols = slice(n * SLOTS + i * 128, n * SLOTS + (i + 1) * 128)
                k = kjt[:, cols]
                k = k * co + jnp.concatenate([k[64:], k[:64]], axis=0) * so
                alive = lane + (place + i * 128) < length
                kkt[:, cols] = jnp.where(alive, k, live_col[...]).astype(BF16)

    def share_rubric(n):
        kkt[n, :, 3 * SLOTS : 3 * SHARD] = kkt[0, :, 3 * SLOTS : 3 * SHARD]

    def flash(slot, keys, kkt, first=False, tiles=range(4)):
        scores = [
            jnp.dot(qbuf[slot, i * 256 : (i + 1) * 256, :], kkt[:, 0:keys], preferred_element_type=F32)
            for i in tiles
        ]
        for s, i in zip(scores, tiles):
            rows = slice(i * 256, (i + 1) * 256)
            top = jnp.max(s, axis=1, keepdims=True) * SCALE
            if first:
                new = jnp.broadcast_to(top, (256, 128))
            else:
                old = peak[slot, rows, :]
                new = jnp.maximum(old, top)
            p = jnp.exp2(s * SCALE - new[:, 0:1]).astype(BF16)
            o = jnp.dot(p, vaug[0:keys, :], preferred_element_type=F32)
            if first:
                acc[slot, rows, :] = o
            else:
                f = jnp.exp2(old - new)
                acc[slot, rows, 0:128] = acc[slot, rows, 0:128] * f + o[:, 0:128]
                acc[slot, rows, 128:256] = acc[slot, rows, 128:256] * f + o[:, 128:256]
            peak[slot, rows, :] = new

    near = (z, zs(-1), zs(1))

    def ordered(n, base):
        return lax.rem(y + base + 3 * n + 3 * lax.div(n, 2) + 2 * lax.div(n, 3), 4)

    one = kkt.at[0]
    prepare(near[:1], one)
    forward(0, 1)
    arrived(qdir)
    start(qfwd)
    forward(0, 0)
    prepare(near[1:], one, 3, 1)

    def unit_near(n, carry):
        slot = ordered(n, 0)

        @pl.when(n == 1)
        def _():
            forward(1, 1)

        @pl.when(n == 2)
        def _():
            forward(1, 0)

        @pl.when(n == 3)
        def _():
            arrived(qfwd)

        rotate(near, slot, one)
        flash(slot, 3 * SHARD, one, True)
        return carry

    lax.fori_loop(0, 4, unit_near, 0)

    forward(2, 1)
    second = (zs(-2), zs(2))
    prepare(second, one, 2)

    def unit_second(n, carry):
        slot = lax.rem(y + n, 4)

        @pl.when(n == 1)
        def _():
            forward(2, 0)

        rotate(second, slot, one)
        flash(slot, 2 * SHARD, one)
        return carry

    lax.fori_loop(0, 4, unit_second, 0)

    eye = lax.broadcasted_iota(jnp.int32, (CHUNK, 128), 0) == lax.broadcasted_iota(jnp.int32, (CHUNK, 128), 1)

    def outgoing(i, n, dev):
        return (
            copy(osend.at[i, n], obuf.at[i, n], os.at[i, n], orr.at[i, n], dev),
            copy(lsend.at[i, n], lbuf.at[i, n], ls.at[i, n], lr.at[i, n], dev),
        )

    def finish(i, n, slot):
        for h in range(GROUP):
            rows = slice(i * HALF + h * CHUNK, i * HALF + (h + 1) * CHUNK)
            total = acc[slot, rows, 128:256]
            stat = peak[slot, rows, :] + jnp.log2(total)
            osend[i, n, h * CHUNK : (h + 1) * CHUNK, :] = (acc[slot, rows, 0:128] / total).astype(BF16)
            lsend[i, n, h : h + 1, :] = jnp.sum(jnp.where(eye, stat, 0.0), axis=0, keepdims=True)

        @pl.when(n != 3)
        def _():
            start(outgoing(i, n, at(slot, z)))

    def last_slot(n):
        return ordered(n, 2)

    partials = [
        [outgoing(i, 0, beyond), outgoing(i, 1, north), outgoing(i, 2, south)] for i in range(2)
    ]

    def combine(i):
        for pair in partials[i]:
            arrived(pair)
        stats = [lbuf[i, 0], lbuf[i, 1], lbuf[i, 2], lsend[i, 3]]
        top = functools.reduce(jnp.maximum, stats)
        parts = [jnp.exp2(s - top) for s in stats]
        total = parts[0] + parts[1] + parts[2] + parts[3]
        shares = [jnp.concatenate([p / total] * 16, axis=0).T for p in parts]
        for h in range(GROUP):
            rows = slice(h * CHUNK, (h + 1) * CHUNK)
            out = None
            for n in range(4):
                src = osend[i, 3, rows, :] if n == 3 else obuf[i, n, rows, :]
                term = shares[n][0:CHUNK, h : h + 1] * src.astype(F32)
                out = term if out is None else out + term
            att[i, :, h * 128 : (h + 1) * 128] = out.astype(BF16)

    half = lax.div(head, 4)
    mine = half == rep
    u = lax.rem(x - 2 * rep + 8, 4)
    g = lax.rem(head, 4)
    far = 1 - rep

    swaps = [
        copy(att.at[i], fbuf.at[g, rep, i], zsend.at[i], zrecv.at[i], partner)
        for i in range(2)
    ]
    swapped = [
        copy(fbuf.at[g, far, i], fbuf.at[g, far, i], zsend.at[i], zrecv.at[i], partner)
        for i in range(2)
    ]

    def block(k, n):
        return fbuf.at[k, rep if n < 2 else far, n % 2]

    def hop(blk, n, way):
        return copy(blk, blk, xs.at[n, way], xr.at[n, way], (east, west)[way])

    def cross(blk, n, way):
        return copy(blk, blk, ds.at[n, way], dr.at[n, way], other)

    def spread(n):
        blk = block(g, n)
        start((hop(blk, n, 0), hop(blk, n, 1), cross(blk, n, 0)))

    def publish(i):
        combine(i)

        @pl.when(mine)
        def _():
            fbuf[g, rep, i] = att[i]
            spread(i)

        @pl.when(jnp.logical_not(mine))
        def _():
            swaps[i].start()

    low, high = core, 2 + core
    roles = ((low, high), (high, low), (high, low), (low, high))

    def collect(n):
        for which, (k0, k1) in enumerate(roles):

            @pl.when(u == which)
            def _():
                if which < 2:
                    blk = block(k1, n)
                    hop(blk, n, 1 - which).wait_recv()
                    cross(blk, n, 1).start()
                else:
                    way = which - 2
                    blk, blk1 = block(k0, n), block(k1, n)
                    hop(blk, n, way).wait_recv()
                    start((copy(blk, blk, fs.at[n], fr.at[n], (east, west)[way]), cross(blk, n, 0)))
                    copy(blk1, blk1, fs.at[n], fr.at[n], (east, west)[way]).wait_recv()
                    cross(blk1, n, 1).start()

    def crossed(n):
        blk = block(g, n)
        cross(blk, n, 0).wait_recv()
        cross(blk, n, 1).wait_recv()

    def product(r, i):
        total = None
        for k in range(4):
            term = jnp.dot(
                fbuf[k, r, i], wbuf[k * 1024 : (k + 1) * 1024, :], preferred_element_type=F32
            )
            total = term if total is None else total + term
        return total

    arrived(rings[3][0])
    arrived(rings[3][1])
    last = (zs(-3), zs(3), zs(4))
    for n in range(4):
        prepare(last, kkt.at[n], 3) if n == 0 else share_rubric(n)

    def unit_last(n, carry):
        slot = last_slot(n)
        rotate(last, slot, kkt.at[n])
        flash(slot, 3 * SHARD, kkt.at[n], tiles=(0, 1))
        finish(0, n, slot)
        return carry

    lax.fori_loop(0, 4, unit_last, 0)

    def unit_end(n, carry):
        slot = last_slot(n)

        @pl.when(n == 2)
        def _():
            publish(0)

        flash(slot, 3 * SHARD, kkt.at[n], tiles=(2, 3))
        finish(1, n, slot)
        return carry

    lax.fori_loop(0, 4, unit_end, 0)
    collect(0)
    publish(1)
    collect(1)
    for c in wload:
        c.wait()
    sends = []
    for i in range(2):

        @pl.when(mine)
        def _():
            swapped[i].wait_recv()
            spread(2 + i)

        collect(2 + i)
        crossed(2 + i)
        part[i] = product(far, i).astype(BF16)
        c = copy(part.at[i], got.at[i], ps.at[i], pr.at[i], partner)
        c.start()
        sends.append(c)
    crossed(0)
    crossed(1)
    own = [product(rep, i) for i in range(2)]
    for i in range(2):
        rows = slice(i * CHUNK, (i + 1) * CHUNK)
        sends[i].wait_recv()
        out_ref[rows, :] = (own[i] + got[i].astype(F32)).astype(BF16)

    for pairs in (*rings, (qdir, qfwd), *partials, (sends,)):
        for pair in pairs:
            for c in pair:
                c.wait_send()
    for n in range(4):
        blk = block(g, n)
        cross(blk, n, 0).wait_send()
        cross(blk, n, 1).wait_send()

    @pl.when(mine)
    def _():
        for n in range(4):
            hop(block(g, n), n, 0).wait_send()
            hop(block(g, n), n, 1).wait_send()

    @pl.when(jnp.logical_not(mine))
    def _():
        for n in range(4):
            blk = block(g, n)
            copy(blk, blk, fs.at[n], fr.at[n], east).wait_send()
        for c in swaps:
            c.wait_send()


VMEM = pl.BlockSpec(memory_space=pltpu.VMEM)
ANY = pl.BlockSpec(memory_space=pl.ANY)
DMA = pltpu.SemaphoreType.DMA


def local(
    queries, criteria_keys, criteria_values, candidate_keys, candidate_values,
    lengths, orders, out_weight,
):
    cos, sin = angle_tables()
    V = pltpu.VMEM
    return pl.pallas_call(
        fused_kernel,
        out_shape=jax.ShapeDtypeStruct((ROWS, 1024), BF16),
        in_specs=[ANY] * 10,
        out_specs=VMEM,
        scratch_shapes=[
            V((1, 16), jnp.int32), V((16, 16), jnp.int32), V((16, 128), jnp.int32), V((4, 16, 128), jnp.int32),
            V((ROWS, 1024), BF16), V((SLOTS, 128), BF16), V((RUB, 128), BF16), V((SLOTS, 128), BF16),
            V((RUB, 128), BF16), V((1024, 128), F32), V((1024, 128), F32),
            V((128, 128), F32), V((128, 128), F32), V((128, 128), F32), V((128, 128), F32), V((128, 128), F32), V((128, 128), F32),
            V((16, 128, 128), F32), V((16, 128, 128), F32),
            V((4, 1024, 128), BF16), V((8, SHARD, 128), BF16), V((8, SHARD, 128), BF16),
            V((128, 3 * SLOTS), F32), V((4, 128, 3 * SHARD), BF16), V((3 * SHARD, 256), BF16), V((128, 128), F32),
            V((4, 1024, 256), F32), V((4, 1024, 128), F32),
            V((2, 4, HALF, 128), BF16), V((2, 4, 8, 128), F32),
            V((2, 4, HALF, 128), BF16), V((2, 4, 8, 128), F32),
            V((4096, 1024), BF16), V((4, 2, 2, CHUNK, 1024), BF16),
            V((2, CHUNK, 1024), BF16), V((2, CHUNK, 1024), BF16), V((2, CHUNK, 1024), BF16),
            DMA((15,)), DMA((4,)),
            DMA((4,)), DMA((4,)),
            DMA((2, 8)), DMA((2, 8)),
            DMA((2, 4)), DMA((2, 4)),
            DMA((2, 4)), DMA((2, 4)),
            DMA((2,)), DMA((2,)),
            DMA((4, 2)), DMA((4, 2)),
            DMA((4,)), DMA((4,)),
            DMA((4, 2)), DMA((4, 2)),
            DMA((2,)), DMA((2,)),
        ],
        compiler_params=pltpu.CompilerParams(
            collective_id=0, has_side_effects=True, vmem_limit_bytes=58 * 1024 * 1024
        ),
        name="judge",
    )(
        queries, criteria_keys, criteria_values, candidate_keys, candidate_values,
        jnp.asarray(cos), jnp.asarray(sin), out_weight, lengths.reshape(1, 16), orders,
    )


def solution(mesh):
    rows = P(("seg", "rep"), "head")
    return jax.shard_map(
        local,
        mesh=mesh,
        in_specs=(rows, rows, rows, rows, rows, P(), P(), P("rep", "head")),
        out_specs=rows,
        check_vma=False,
    )
```
